512 devices in a mesh: dp: 64 (over x, z, core), mp: 8 (over y).
Axes of the slice: x: 4, y: 8, z: 8, core: 2. Of those that a mesh axis runs over, the one named last changes fastest.
Arguments:
- activations: bfloat16 [65536, 12288], P('dp', 'mp'), may hold values from -40 to 40
- output_grads: bfloat16 [65536, 512], P('dp', 'mp'), may hold values from -2.5 to 2.5
- master: float32 [512, 12288], P('mp', 'dp'), may hold values from -0.12 to 0.12
- moment_q: bfloat16 [512, 12288], P('mp', 'dp'), may hold values from -1 to 1
- moment_range: float32 [1], replicated, may hold values from 0.01 to 0.05
- second_moment: float32 [512, 12288], P('mp', 'dp'), may hold values from 0.0001 to 0.03
Outputs:
- master_new: float32 [512, 12288], P('mp', 'dp')
- moment_q_new: bfloat16 [512, 12288], P('mp', 'dp')
- moment_range_new: float32 [1], replicated
- second_new: float32 [512, 12288], P('mp', 'dp')
- weight_q: bfloat16 [512, 12288], P('mp')
- weight_range: float32 [1], replicated
- grad_range: float32 [1], replicated
The draws below stay inside these ranges and needn't reach their ends.
All inputs are finite; a program needn't handle non-finite values. Where the reference program divides by a largest or mean magnitude, that divisor is 1e-20 or more.
Results may differ from the reference program's by a relative error of at most 0.0051.
Values may be sent and summed in bfloat16 or wider, within the bound.
No kernel may reach another device: no remote copies, remote signals or barrier semaphores. Data moves between devices by JAX's collectives and lax.ppermute only.
A program may use at most 64 MiB of HBM per device.

```python
import math
import jax
import jax.numpy as jnp
from jax import lax

D = 12288
TOK = 1024
TOKENS = 65536
COLS_ALL = 512
N_DP = 64
N_MP = 8


def block_scales(key, length, blocks, factor, keep_lower):
    width = length // blocks
    if keep_lower:
        lower_count = blocks // 2
        shuffled = jax.random.permutation(key, blocks - lower_count).astype(jnp.int32)
        ranking = jnp.concatenate([jnp.arange(lower_count, dtype=jnp.int32), lower_count + shuffled])
    else:
        ranking = jax.random.permutation(key, blocks).astype(jnp.int32)
    levels = ranking.astype(jnp.float32) / max(blocks - 1, 1)
    return jnp.repeat(jnp.exp(jnp.log(factor) * levels), width)


def draw_activations(key, part):
    key = jax.random.fold_in(key, 11)
    order_key = jax.random.fold_in(key, 70)
    noise = jax.random.truncated_normal(key, -4.0, 4.0, (TOKENS, D), jnp.float32)
    feature_scale = block_scales(order_key, D, N_DP, 10.0, True)
    return (noise * feature_scale[None, :]).astype(jnp.bfloat16)


def draw_output_grads(key, part):
    key = jax.random.fold_in(key, 23)
    order_key = jax.random.fold_in(key, 60)
    noise = jax.random.truncated_normal(key, -4.0, 4.0, (TOKENS, COLS_ALL), jnp.float32)
    token_scale = block_scales(jax.random.fold_in(order_key, 1), TOKENS, N_DP, 10.0, True)
    column_scale = block_scales(jax.random.fold_in(order_key, 2), COLS_ALL, N_MP, 3.0, False)
    scaled = noise * 0.02 * token_scale[:, None] * column_scale[None, :]
    return scaled.astype(jnp.bfloat16)


def draw_master(key, part):
    key = jax.random.fold_in(key, 37)
    order_key = jax.random.fold_in(key, 80)
    noise = jax.random.truncated_normal(key, -4.0, 4.0, (COLS_ALL, D), jnp.float32)
    column_scale = block_scales(jax.random.fold_in(order_key, 1), COLS_ALL, N_MP, 3.0, False)
    feature_scale = block_scales(jax.random.fold_in(order_key, 2), D, N_DP, 10.0, True)
    return noise * 0.001 * column_scale[:, None] * feature_scale[None, :]


def draw_moment_q(key, part):
    key = jax.random.fold_in(key, 41)
    order_key = jax.random.fold_in(key, 90)
    noise = jax.random.uniform(key, (COLS_ALL, D), jnp.float32, -1.0, 1.0)
    column_scale = block_scales(jax.random.fold_in(order_key, 1), COLS_ALL, N_MP, 3.0, False)
    feature_scale = block_scales(jax.random.fold_in(order_key, 2), D, N_DP, 10.0, True)
    scaled = noise * (column_scale[:, None] / 3.0) * (feature_scale[None, :] / 10.0)
    return scaled.astype(jnp.bfloat16)


def level_of(own_key, dims, cuts, low, high):
    level, own = 1.0, jax.random.fold_in(own_key, 6)
    for position, parts in cuts:
        steps = jnp.exp(jax.random.uniform(jax.random.fold_in(own, position), (parts,), jnp.float32, low / len(cuts), high / len(cuts)))
        level = level * jnp.repeat(steps, dims[position] // parts).reshape([-1 if axis == position else 1 for axis in range(len(dims))])
    return level


def setup_inputs(seed: int = 0) -> dict:
    key_list = jax.random.split(jax.random.key(seed), 7)
    return {
        "activations": draw_activations(jax.random.fold_in(key_list[6], 71), 0),
        "output_grads": draw_output_grads(jax.random.fold_in(key_list[6], 71), 0),
        "master": draw_master(jax.random.fold_in(key_list[6], 71), 0),
        "moment_q": draw_moment_q(jax.random.fold_in(key_list[6], 71), 0),
        "moment_range": jnp.clip(jnp.exp(jax.random.uniform(key_list[4], (1,), jnp.float32, math.log(0.01), math.log(0.05))), 0.01, 0.05),
        "second_moment": jnp.clip(jnp.exp(math.log(0.03) - 5.7037825 * jax.random.uniform(key_list[5], (COLS_ALL, D), jnp.float32) ** level_of(key_list[5], (COLS_ALL, D), ((0, 8), (1, 64)), -0.2, 0.2)), 0.0001, 0.03),
    }


EPSILON = 1e-06
BETA_ONE = 0.9
BETA_TWO = 0.999
LEARN_RATE = 0.001
DECAY_RATE = 0.1
ADAM_EPSILON = 1e-08

def rank_gradient(activations, output_grads, index):
    offset = (index * TOK).astype(jnp.int32)
    token_rows = lax.dynamic_slice_in_dim(activations, offset, TOK, 0)
    grad_rows = lax.dynamic_slice_in_dim(output_grads, offset, TOK, 0)
    return jnp.dot(grad_rows.T, token_rows, preferred_element_type=jnp.float32)

def reference(activations, output_grads, master, moment_q, moment_range, second_moment):
    indices = jnp.arange(N_DP, dtype=jnp.int32)

    def find_largest(carry, index):
        partial_value = rank_gradient(activations, output_grads, index)
        return (jnp.maximum(carry, jnp.max(jnp.abs(partial_value))), None)
    largest, _ = lax.scan(find_largest, jnp.zeros((), jnp.float32), indices)
    grad_range = largest + EPSILON

    def add_scaled(carry, index):
        partial_value = rank_gradient(activations, output_grads, index)
        scaled = (partial_value / grad_range).astype(jnp.bfloat16)
        return (carry + scaled.astype(jnp.float32), None)
    summed, _ = lax.scan(add_scaled, jnp.zeros((COLS_ALL, D), jnp.float32), indices)
    gradient = summed * grad_range / N_DP
    moment = BETA_ONE * (moment_q.astype(jnp.float32) * moment_range[0]) + (1.0 - BETA_ONE) * gradient
    second_new = BETA_TWO * second_moment + (1.0 - BETA_TWO) * gradient * gradient
    master_new = master - LEARN_RATE * (moment / (jnp.sqrt(second_new) + ADAM_EPSILON) + DECAY_RATE * master)
    moment_span = jnp.max(jnp.abs(moment)) + EPSILON
    weight_span = jnp.max(jnp.abs(master_new)) + EPSILON
    moment_q_new = (moment / moment_span).astype(jnp.bfloat16)
    weight_q = (master_new / weight_span).astype(jnp.bfloat16)
    return (master_new, moment_q_new, jnp.reshape(moment_span, (1,)), second_new, weight_q, jnp.reshape(weight_span, (1,)), jnp.reshape(grad_range, (1,)))
```

```python
import functools

import jax
import jax.numpy as jnp
from jax import lax
from jax.experimental import pallas as pl
from jax.experimental.pallas import tpu as pltpu
from jax.sharding import Mesh, PartitionSpec as P

EPSILON = 1e-06
BETA_ONE = 0.9
BETA_TWO = 0.999
LEARN_RATE = 0.001
DECAY_RATE = 0.1
ADAM_EPSILON = 1e-08

F32 = jnp.float32
BF16 = jnp.bfloat16
LANES = 128
MAX_ROWS = 16
DEVICE = ("x", "z", "core", "y")


def pack(block):
    half = block.shape[0] // 2
    tail = block[:, LANES:]
    return jnp.concatenate([block[:, :LANES], jnp.concatenate([tail[:half], tail[half:]], 1)], 0)


def unpack(packed, rows):
    tail = packed[rows:]
    tail = jnp.concatenate([tail[:, : LANES // 2], tail[:, LANES // 2 :]], 0)
    return jnp.concatenate([packed[:rows], tail], 1)


def add_and_cut(parts_ref, out_ref):
    total = parts_ref[0].astype(F32)
    for part in range(1, parts_ref.shape[0]):
        total += parts_ref[part].astype(F32)
    width = total.shape[1] // out_ref.shape[0]
    for piece in range(out_ref.shape[0]):
        out_ref[piece] = pack(total[:, piece * width : (piece + 1) * width]).astype(BF16)


def largest(value):
    return jnp.max(jnp.max(jnp.abs(value), axis=1, keepdims=True), axis=0, keepdims=True)


def adam_step(
    devices, summed_ref, partial_ref, range_ref, master_ref, moment_ref, second_ref,
    master_out, second_out, moment_out, sent_out,
):
    rows = master_ref.shape[0]
    gradient = unpack(summed_ref[...], rows) / devices
    moment = (
        BETA_ONE * (moment_ref[...].astype(F32) * range_ref[0]) + (1.0 - BETA_ONE) * gradient
    )
    second_new = BETA_TWO * second_ref[...] + (1.0 - BETA_TWO) * gradient * gradient
    master = master_ref[...]
    master_new = master - LEARN_RATE * (
        moment / (jnp.sqrt(second_new) + ADAM_EPSILON) + DECAY_RATE * master
    )
    master_out[...] = master_new
    second_out[...] = second_new
    moment_out[...] = moment
    packed = pack(master_new)
    sent_out[: packed.shape[0]] = packed.astype(BF16)
    row = lax.broadcasted_iota(jnp.int32, (MAX_ROWS, LANES), 0)
    spread = jnp.zeros((MAX_ROWS, LANES), F32)
    tops = (jnp.full((1, 1), partial_ref[0], F32), largest(moment), largest(master_new))
    for place, top in enumerate(tops):
        rest = jnp.broadcast_to(top, (MAX_ROWS, LANES))
        for piece in range(3):
            rounded = rest.astype(BF16).astype(F32)
            spread = jnp.where(row == 3 * place + piece, rounded, spread)
            rest = rest - rounded
    sent_out[packed.shape[0] :] = spread.astype(BF16)


def find_tops(own_ref, other_ref, out_ref):
    held = jnp.concatenate([own_ref[...], other_ref[...]], 0).astype(F32)
    best = [None] * 3
    for block in range(held.shape[0]):
        for place in range(3):
            row = 3 * place
            top = held[block, row : row + 1] + held[block, row + 1 : row + 2] + held[block, row + 2 : row + 3]
            best[place] = top if best[place] is None else jnp.maximum(best[place], top)
    out_ref[...] = jnp.concatenate(best + [jnp.zeros((5, LANES), F32)], 0)


def scale_weights(core_ref, spans_ref, own_ref, other_ref, moment_ref, weight_out, moment_out):
    rows = weight_out.shape[0]
    is_first = core_ref[0] == 0
    span = spans_ref[2]

    @pl.when(pl.program_id(0) == 0)
    def _():
        moment_out[...] = (moment_ref[...] / spans_ref[1]).astype(BF16)

    used = rows + rows // 2
    for place in range(own_ref.shape[1]):
        own = own_ref[0, place, :used].astype(F32)
        other = other_ref[0, place, :used].astype(F32)
        first = unpack(jnp.where(is_first, own, other), rows)
        second = unpack(jnp.where(is_first, other, own), rows)
        pair = jnp.concatenate([first, second], 1) / span
        width = pair.shape[1]
        weight_out[:, place * width : (place + 1) * width] = pair.astype(BF16)


def copies_to_all(value, axis):
    copies = jnp.broadcast_to(value[None], (lax.axis_size(axis), *value.shape))
    return lax.all_to_all(copies, axis, 0, 0, tiled=True)


def on_device(activations, output_grads, master, moment_q, moment_range, second_moment):
    xs, zs, cores, ys = (lax.axis_size(name) for name in DEVICE)
    rows, width = master.shape
    packed_rows = rows + rows // 2
    sent_rows = packed_rows + MAX_ROWS
    smem = pl.BlockSpec(memory_space=pltpu.SMEM)
    vmem = pl.BlockSpec(memory_space=pltpu.VMEM)

    gathered = copies_to_all(output_grads.T, "y").reshape(-1, output_grads.shape[0])
    partial_value = jnp.dot(gathered, activations, preferred_element_type=F32)
    partial_top = jnp.max(jnp.abs(partial_value))

    value = partial_value.astype(BF16).reshape(cores, -1, partial_value.shape[1])
    value = lax.all_to_all(value, "core", 0, 0, tiled=True)
    value = jnp.sum(value.astype(F32), axis=0).astype(BF16)
    value = lax.all_to_all(value.reshape(xs, rows, -1), "x", 0, 0, tiled=True)
    value = pl.pallas_call(
        add_and_cut,
        out_shape=jax.ShapeDtypeStruct((zs, packed_rows, LANES), BF16),
        in_specs=[vmem],
        out_specs=vmem,
    )(value)
    value = lax.all_to_all(value, "z", 0, 0, tiled=True)
    value = jnp.sum(value.astype(F32), axis=0)
    route = []
    for x in range(xs):
        for z in range(zs):
            for core in range(cores):
                for y in range(ys):
                    source = ((x * zs + z) * cores + core) * ys + y
                    route.append((source, (y * zs + z) * ys + core * xs + x))
    value = lax.ppermute(value, DEVICE, route)

    block = jax.ShapeDtypeStruct((rows, width), F32)
    master_new, second_new, moment, sent = pl.pallas_call(
        functools.partial(adam_step, xs * zs * cores),
        out_shape=(block, block, block, jax.ShapeDtypeStruct((sent_rows, LANES), BF16)),
        in_specs=[vmem, smem, smem, vmem, vmem, vmem],
        out_specs=(vmem,) * 4,
    )(value, partial_top.reshape(1), moment_range, master, moment_q, second_moment)

    held = copies_to_all(sent, "z")
    held = copies_to_all(held, "x").reshape(xs, zs, sent_rows, LANES)
    other = lax.ppermute(held, "core", [(0, 1), (1, 0)])
    tops = pl.pallas_call(
        find_tops,
        out_shape=jax.ShapeDtypeStruct((8, LANES), F32),
        in_specs=[vmem, vmem],
        out_specs=vmem,
    )(
        held[:, :, packed_rows:].reshape(xs * zs, MAX_ROWS, LANES),
        other[:, :, packed_rows:].reshape(xs * zs, MAX_ROWS, LANES),
    )
    spans = lax.pmax(tops[:3, 0], "y") + EPSILON

    group = (1, zs, sent_rows, LANES)
    weight_q, moment_q_new = pl.pallas_call(
        scale_weights,
        grid=(xs,),
        out_shape=(
            jax.ShapeDtypeStruct((rows, width * xs * zs * cores), BF16),
            jax.ShapeDtypeStruct((rows, width), BF16),
        ),
        in_specs=[
            smem,
            smem,
            pl.BlockSpec(group, lambda i: (i, 0, 0, 0)),
            pl.BlockSpec(group, lambda i: (i, 0, 0, 0)),
            pl.BlockSpec((rows, width), lambda i: (0, 0)),
        ],
        out_specs=(
            pl.BlockSpec((rows, width * zs * cores), lambda i: (0, i)),
            pl.BlockSpec((rows, width), lambda i: (0, 0)),
        ),
    )(lax.axis_index("core").reshape(1), spans, held, other, moment)
    return (
        master_new,
        moment_q_new,
        spans[1:2],
        second_new,
        weight_q,
        spans[2:3],
        spans[0:1],
    )


def solution(mesh):
    inner = Mesh(mesh.devices.reshape(4, 8, 2, 8), DEVICE)
    dp, mp = ("x", "z", "core"), "y"
    placed = (P(dp, mp), P(dp, mp), P(mp, dp), P(mp, dp), P(), P(mp, dp))
    return jax.shard_map(
        on_device,
        mesh=inner,
        in_specs=placed,
        out_specs=(P(mp, dp), P(mp, dp), P(), P(mp, dp), P(mp, None), P(), P()),
        check_vma=False,
    )
```

```python
import functools

import jax
import jax.numpy as jnp
from jax import lax
from jax.experimental import pallas as pl
from jax.experimental.pallas import tpu as pltpu
from jax.sharding import Mesh, PartitionSpec as P

EPSILON = 1e-06
BETA_ONE = 0.9
BETA_TWO = 0.999
LEARN_RATE = 0.001
DECAY_RATE = 0.1
ADAM_EPSILON = 1e-08

F32 = jnp.float32
BF16 = jnp.bfloat16
LANES = 128
HALF = LANES // 2
TOP_ROWS = 16
TILE = 512
DEVICE = ("x", "z", "core", "y")
SMEM = pl.BlockSpec(memory_space=pltpu.SMEM)
VMEM = pl.BlockSpec(memory_space=pltpu.VMEM)
PARAMS = pltpu.CompilerParams(vmem_limit_bytes=32 * 1024 * 1024)


def fold(middle, odd):
    rows = middle.shape[0] // 2
    upper, lower = middle[:rows], pltpu.roll(middle[rows:], HALF, 1)
    left = lax.broadcasted_iota(jnp.int32, upper.shape, 1) < HALF
    return jnp.where(left, lower, upper) if odd else jnp.where(left, upper, lower)


def unfold(even_tail, odd_tail):
    left = lax.broadcasted_iota(jnp.int32, even_tail.shape, 1) < HALF
    upper = jnp.where(left, even_tail, odd_tail)
    lower = pltpu.roll(jnp.where(left, odd_tail, even_tail), HALF, 1)
    return jnp.concatenate([upper, lower], 0)


def largest(value):
    return jnp.max(jnp.max(jnp.abs(value), axis=1, keepdims=True), axis=0, keepdims=True)


def multiply_for_other(core_ref, grads_ref, activations_ref, out_ref, top_ref):
    grads = grads_ref[1 - core_ref[0]]
    best = None
    for start in range(0, out_ref.shape[1], TILE):
        value = jnp.dot(grads, activations_ref[:, start : start + TILE], preferred_element_type=F32)
        out_ref[:, start : start + TILE] = value.astype(BF16)
        best = largest(value) if best is None else jnp.maximum(best, largest(value))
    top_ref[...] = jnp.broadcast_to(best, top_ref.shape)


def multiply_and_add(core_ref, grads_ref, activations_ref, other_ref, out_ref, top_ref):
    grads = grads_ref[core_ref[0]]
    best = None
    for start in range(0, out_ref.shape[1], TILE):
        value = jnp.dot(grads, activations_ref[:, start : start + TILE], preferred_element_type=F32)
        out_ref[:, start : start + TILE] = (
            value + other_ref[:, start : start + TILE].astype(F32)
        ).astype(BF16)
        best = largest(value) if best is None else jnp.maximum(best, largest(value))
    top_ref[...] = jnp.broadcast_to(best, top_ref.shape)


def add_and_cut(parts_ref, out_ref):
    rows = parts_ref.shape[1]

    def total(tile):
        where = slice(tile * LANES, (tile + 1) * LANES)
        value = parts_ref[0, :, where].astype(F32)
        for part in range(1, parts_ref.shape[0]):
            value += parts_ref[part, :, where].astype(F32)
        return value

    for pair in range(out_ref.shape[0] // 2):
        middle = total(3 * pair + 1)
        for odd in range(2):
            out_ref[2 * pair + odd, :rows] = total(3 * pair + 2 * odd).astype(BF16)
            out_ref[2 * pair + odd, rows:] = fold(middle, odd).astype(BF16)


def adam_step(
    devices, core_ref, range_ref, summed_ref, first_top_ref, second_top_ref,
    master_ref, moment_ref, second_ref,
    master_out, second_out, moment_out, sent_out, tops_out,
):
    rows = master_ref.shape[0]
    is_even = core_ref[0] == 0
    own, tail = summed_ref[:rows], summed_ref[rows:]
    middle = unfold(tail, tail)
    gradient = jnp.where(
        is_even,
        jnp.concatenate([own, middle[:, :HALF]], 1),
        jnp.concatenate([middle[:, HALF:], own], 1),
    ) / devices
    moment = (
        BETA_ONE * (moment_ref[...].astype(F32) * range_ref[0]) + (1.0 - BETA_ONE) * gradient
    )
    second_new = BETA_TWO * second_ref[...] + (1.0 - BETA_TWO) * gradient * gradient
    master = master_ref[...]
    master_new = master - LEARN_RATE * (
        moment / (jnp.sqrt(second_new) + ADAM_EPSILON) + DECAY_RATE * master
    )
    master_out[...] = master_new
    second_out[...] = second_new
    moment_out[...] = moment
    sent_out[:rows] = jnp.where(is_even, master_new[:, :LANES], master_new[:, HALF:]).astype(BF16)
    middle = jnp.concatenate([master_new[:, LANES:], master_new[:, :HALF]], 1)
    sent_out[rows:] = jnp.where(is_even, fold(middle, False), fold(middle, True)).astype(BF16)
    row = lax.broadcasted_iota(jnp.int32, (8, LANES), 0)
    partial_top = jnp.maximum(first_top_ref[...], second_top_ref[...])
    tops = jnp.where(row == 0, partial_top, jnp.where(row == 1, largest(moment), largest(master_new)))
    for copy in range(tops_out.shape[0]):
        tops_out[copy] = tops


def join_tops(tops_ref, weights_ref, out_ref):
    rows = weights_ref.shape[0]
    top = tops_ref[0]
    for place in range(1, tops_ref.shape[0]):
        top = jnp.maximum(top, tops_ref[place])
    high = top.astype(BF16).astype(F32)
    middle = (top - high).astype(BF16).astype(F32)
    low = top - high - middle
    row = lax.broadcasted_iota(jnp.int32, top.shape, 0)
    spread = jnp.concatenate([jnp.where(row < 4, high, pltpu.roll(low, 4, 0)), middle], 0)
    for copy in range(out_ref.shape[0]):
        out_ref[copy, :rows] = weights_ref[...]
        out_ref[copy, rows:] = spread.astype(BF16)


def scale_weights(
    core_ref, own_ref, other_ref, moment_ref,
    weight_out, moment_out, moment_span_out, weight_span_out, grad_span_out, span_ref,
):
    rows = weight_out.shape[0]
    packed = rows + rows // 2
    step = pl.program_id(0)
    is_even = core_ref[0] == 0

    @pl.when(step == 0)
    def _():
        best = jnp.zeros((8, LANES), F32)
        for held in (own_ref, other_ref):
            for x in range(held.shape[0]):
                for z in range(held.shape[1]):
                    spread = held[x, z, packed:].astype(F32)
                    high, middle = spread[:8], spread[8:]
                    best = jnp.maximum(best, high + middle + pltpu.roll(high, 4, 0))
        spans = best + EPSILON
        span_ref[...] = spans
        moment_out[...] = (moment_ref[...] / largest(spans[1:2])).astype(BF16)
        grad_span_out[0] = jnp.max(spans[0:1])
        moment_span_out[0] = jnp.max(spans[1:2])
        weight_span_out[0] = jnp.max(spans[2:3])

    span = span_ref[2:3]
    for place in range(own_ref.shape[1]):
        own = own_ref[step, place, :packed].astype(F32) / span
        other = other_ref[step, place, :packed].astype(F32) / span
        even, odd = jnp.where(is_even, own, other), jnp.where(is_even, other, own)
        start = 3 * LANES * place
        weight_out[:, start : start + LANES] = even[:rows].astype(BF16)
        weight_out[:, start + LANES : start + 2 * LANES] = unfold(even[rows:], odd[rows:]).astype(BF16)
        weight_out[:, start + 2 * LANES : start + 3 * LANES] = odd[:rows].astype(BF16)


def copies_to_all(value, axis):
    copies = jnp.broadcast_to(value[None], (lax.axis_size(axis), *value.shape))
    return lax.all_to_all(copies, axis, 0, 0, tiled=True)


def on_device(activations, output_grads, master, moment_q, moment_range, second_moment):
    xs, zs, cores, ys = (lax.axis_size(name) for name in DEVICE)
    rows, width = master.shape
    packed = rows + rows // 2
    sent_rows = packed + TOP_ROWS
    core = lax.axis_index("core").reshape(1)
    swap = [(0, 1), (1, 0)]

    grads = copies_to_all(output_grads.T, "y").reshape(cores, -1, output_grads.shape[0])
    product = (
        jax.ShapeDtypeStruct((grads.shape[1], activations.shape[1]), BF16),
        jax.ShapeDtypeStruct((8, LANES), F32),
    )
    value, first_top = pl.pallas_call(
        multiply_for_other,
        out_shape=product,
        in_specs=[SMEM, VMEM, VMEM],
        out_specs=(VMEM, VMEM),
        compiler_params=PARAMS,
    )(core, grads, activations)

    value = lax.ppermute(value, "core", swap)
    value, second_top = pl.pallas_call(
        multiply_and_add,
        out_shape=product,
        in_specs=[SMEM, VMEM, VMEM, VMEM],
        out_specs=(VMEM, VMEM),
        compiler_params=PARAMS,
    )(core, grads, activations, value)
    value = lax.all_to_all(value.reshape(xs, rows, -1), "x", 0, 0, tiled=True)
    value = pl.pallas_call(
        add_and_cut,
        out_shape=jax.ShapeDtypeStruct((zs, packed, LANES), BF16),
        in_specs=[VMEM],
        out_specs=VMEM,
    )(value)
    value = lax.all_to_all(value, "z", 0, 0, tiled=True)
    value = jnp.sum(value.astype(F32), axis=0)
    route = []
    for x in range(xs):
        for z in range(zs):
            for half in range(cores):
                for y in range(ys):
                    source = ((x * zs + z) * cores + half) * ys + y
                    route.append((source, (y * zs + z) * ys + half * xs + x))
    value = lax.ppermute(value, DEVICE, route)

    block = jax.ShapeDtypeStruct((rows, width), F32)
    master_new, second_new, moment, weights, tops = pl.pallas_call(
        functools.partial(adam_step, xs * zs * cores),
        out_shape=(
            block,
            block,
            block,
            jax.ShapeDtypeStruct((packed, LANES), BF16),
            jax.ShapeDtypeStruct((ys, 8, LANES), F32),
        ),
        in_specs=[SMEM, SMEM] + [VMEM] * 6,
        out_specs=(VMEM,) * 5,
    )(core, moment_range, value, first_top, second_top, master, moment_q, second_moment)

    tops = lax.all_to_all(tops, "y", 0, 0, tiled=True)
    held = pl.pallas_call(
        join_tops,
        out_shape=jax.ShapeDtypeStruct((zs, sent_rows, LANES), BF16),
        in_specs=[VMEM, VMEM],
        out_specs=VMEM,
    )(tops, weights)
    held = lax.all_to_all(held, "z", 0, 0, tiled=True)
    held = copies_to_all(held, "x").reshape(xs, zs, sent_rows, LANES)
    other = lax.ppermute(held, "core", swap)

    one = jax.ShapeDtypeStruct((1,), F32)
    weight_q, moment_q_new, moment_span, weight_span, grad_span = pl.pallas_call(
        scale_weights,
        grid=(xs,),
        out_shape=(
            jax.ShapeDtypeStruct((rows, width * xs * zs * cores), BF16),
            jax.ShapeDtypeStruct((rows, width), BF16),
            one,
            one,
            one,
        ),
        in_specs=[SMEM, VMEM, VMEM, VMEM],
        out_specs=(
            pl.BlockSpec((rows, width * zs * cores), lambda i: (0, i)),
            VMEM,
            SMEM,
            SMEM,
            SMEM,
        ),
        scratch_shapes=[pltpu.VMEM((8, LANES), F32)],
        compiler_params=PARAMS,
    )(core, held, other, moment)
    return master_new, moment_q_new, moment_span, second_new, weight_q, weight_span, grad_span


def solution(mesh):
    inner = Mesh(mesh.devices.reshape(4, 8, 2, 8), DEVICE)
    dp, mp = ("x", "z", "core"), "y"
    placed = (P(dp, mp), P(dp, mp), P(mp, dp), P(mp, dp), P(), P(mp, dp))
    return jax.shard_map(
        on_device,
        mesh=inner,
        in_specs=placed,
        out_specs=(P(mp, dp), P(mp, dp), P(), P(mp, dp), P(mp, None), P(), P()),
        check_vma=False,
    )
```

```python
import functools

import jax
import jax.numpy as jnp
from jax import lax
from jax.experimental import pallas as pl
from jax.experimental.pallas import tpu as pltpu
from jax.sharding import Mesh, PartitionSpec as P

EPSILON = 1e-06
BETA_ONE = 0.9
BETA_TWO = 0.999
LEARN_RATE = 0.001
DECAY_RATE = 0.1
ADAM_EPSILON = 1e-08

F32 = jnp.float32
BF16 = jnp.bfloat16
LANES = 128
HALF = LANES // 2
TOP_ROWS = 16
TILE = 512
DEVICE = ("x", "z", "core", "y")
SMEM = pl.BlockSpec(memory_space=pltpu.SMEM)
VMEM = pl.BlockSpec(memory_space=pltpu.VMEM)
PARAMS = pltpu.CompilerParams(vmem_limit_bytes=12 * 1024 * 1024)


def fold(middle, odd):
    rows = middle.shape[0] // 2
    upper, lower = middle[:rows], pltpu.roll(middle[rows:], HALF, 1)
    left = lax.broadcasted_iota(jnp.int32, upper.shape, 1) < HALF
    return jnp.where(left, lower, upper) if odd else jnp.where(left, upper, lower)


def unfold(even_tail, odd_tail):
    left = lax.broadcasted_iota(jnp.int32, even_tail.shape, 1) < HALF
    upper = jnp.where(left, even_tail, odd_tail)
    lower = pltpu.roll(jnp.where(left, odd_tail, even_tail), HALF, 1)
    return jnp.concatenate([upper, lower], 0)


def largest(value):
    return jnp.max(jnp.max(jnp.abs(value), axis=1, keepdims=True), axis=0, keepdims=True)


def magnitude(value, best):
    top = jnp.max(jnp.abs(value).reshape(-1, 8, value.shape[1]), axis=0)
    for start in range(0, value.shape[1], LANES):
        part = top[:, start : start + LANES]
        best = part if best is None else jnp.maximum(best, part)
    return best


def multiply_for_other(core_ref, grads_ref, activations_ref, out_ref, top_ref):
    grads = grads_ref[1 - core_ref[0]]
    best = None
    for start in range(0, out_ref.shape[1], TILE):
        where = slice(start, start + TILE)
        value = jnp.dot(grads, activations_ref[:, where], preferred_element_type=F32)
        out_ref[:, where] = value.astype(BF16)
        best = magnitude(value, best)
    top_ref[...] = best


def multiply_and_add(core_ref, grads_ref, activations_ref, other_ref, first_ref, out_ref, top_ref):
    grads = grads_ref[core_ref[0]]
    best = first_ref[...]
    for start in range(0, out_ref.shape[1], TILE):
        where = slice(start, start + TILE)
        value = jnp.dot(grads, activations_ref[:, where], preferred_element_type=F32)
        out_ref[:, where] = (value + other_ref[:, where].astype(F32)).astype(BF16)
        best = magnitude(value, best)
    top_ref[...] = best


def add_and_cut(parts_ref, out_ref):
    rows = parts_ref.shape[1]

    def total(tile):
        where = slice(tile * LANES, (tile + 1) * LANES)
        value = parts_ref[0, :, where].astype(F32)
        for part in range(1, parts_ref.shape[0]):
            value += parts_ref[part, :, where].astype(F32)
        return value

    for pair in range(out_ref.shape[0] // 2):
        middle = total(3 * pair + 1)
        for odd in range(2):
            out_ref[2 * pair + odd, :rows] = total(3 * pair + 2 * odd).astype(BF16)
            out_ref[2 * pair + odd, rows:] = fold(middle, odd).astype(BF16)


def adam_step(
    devices, core_ref, range_ref, summed_ref, top_ref, master_ref, moment_ref, second_ref,
    master_out, second_out, moment_out, sent_out,
):
    rows = master_ref.shape[0]
    is_even = core_ref[0] == 0
    own, tail = summed_ref[:rows], summed_ref[rows:]
    middle = unfold(tail, tail)
    gradient = jnp.where(
        is_even,
        jnp.concatenate([own, middle[:, :HALF]], 1),
        jnp.concatenate([middle[:, HALF:], own], 1),
    ) / devices
    moment = (
        BETA_ONE * (moment_ref[...].astype(F32) * range_ref[0]) + (1.0 - BETA_ONE) * gradient
    )
    second_new = BETA_TWO * second_ref[...] + (1.0 - BETA_TWO) * gradient * gradient
    master = master_ref[...]
    master_new = master - LEARN_RATE * (
        moment / (jnp.sqrt(second_new) + ADAM_EPSILON) + DECAY_RATE * master
    )
    master_out[...] = master_new
    second_out[...] = second_new
    moment_out[...] = moment
    own = jnp.where(is_even, master_new[:, :LANES], master_new[:, HALF:]).astype(BF16)
    middle = jnp.concatenate([master_new[:, LANES:], master_new[:, :HALF]], 1)
    tail = jnp.where(is_even, fold(middle, False), fold(middle, True)).astype(BF16)
    row = lax.broadcasted_iota(jnp.int32, (8, LANES), 0)
    tops = (largest(top_ref[...]), largest(moment), largest(master_new))
    top = jnp.where(row == 0, tops[0], jnp.where(row == 1, tops[1], tops[2]))
    high = top.astype(BF16).astype(F32)
    middle = (top - high).astype(BF16).astype(F32)
    low = top - high - middle
    spread = jnp.concatenate([jnp.where(row < 4, high, pltpu.roll(low, 4, 0)), middle], 0)
    for copy in range(sent_out.shape[0]):
        sent_out[copy, :rows] = own
        sent_out[copy, rows : rows + rows // 2] = tail
        sent_out[copy, rows + rows // 2 :] = spread.astype(BF16)


def join_tops(held_ref, out_ref):
    packed = held_ref.shape[2] - TOP_ROWS
    best = jnp.zeros((8, LANES), F32)
    for x in range(held_ref.shape[0]):
        for z in range(held_ref.shape[1]):
            spread = held_ref[x, z, packed:].astype(F32)
            high, middle = spread[:8], spread[8:]
            best = jnp.maximum(best, high + middle + pltpu.roll(high, 4, 0))
    for copy in range(out_ref.shape[0]):
        out_ref[copy] = best


def scale_weights(
    core_ref, tops_ref, own_ref, other_ref, moment_ref,
    weight_out, moment_out, moment_span_out, weight_span_out, grad_span_out, span_ref,
):
    rows = weight_out.shape[0]
    packed = rows + rows // 2
    step = pl.program_id(0)
    is_even = core_ref[0] == 0

    @pl.when(step == 0)
    def _():
        best = tops_ref[0]
        for place in range(1, tops_ref.shape[0]):
            best = jnp.maximum(best, tops_ref[place])
        spans = best + EPSILON
        span_ref[...] = spans
        moment_out[...] = (moment_ref[...] / largest(spans[1:2])).astype(BF16)
        grad_span_out[0] = jnp.max(spans[0:1])
        moment_span_out[0] = jnp.max(spans[1:2])
        weight_span_out[0] = jnp.max(spans[2:3])

    span = span_ref[2:3]
    for place in range(own_ref.shape[1]):
        own = own_ref[step, place, :packed].astype(F32) / span
        other = other_ref[step, place, :packed].astype(F32) / span
        even, odd = jnp.where(is_even, own, other), jnp.where(is_even, other, own)
        start = 3 * LANES * place
        weight_out[:, start : start + LANES] = even[:rows].astype(BF16)
        weight_out[:, start + LANES : start + 2 * LANES] = unfold(even[rows:], odd[rows:]).astype(BF16)
        weight_out[:, start + 2 * LANES : start + 3 * LANES] = odd[:rows].astype(BF16)


def copies_to_all(value, axis):
    copies = jnp.broadcast_to(value[None], (lax.axis_size(axis), *value.shape))
    return lax.all_to_all(copies, axis, 0, 0, tiled=True)


def on_device(activations, output_grads, master, moment_q, moment_range, second_moment):
    xs, zs, cores, ys = (lax.axis_size(name) for name in DEVICE)
    rows, width = master.shape
    packed = rows + rows // 2
    sent_rows = packed + TOP_ROWS
    core = lax.axis_index("core").reshape(1)
    swap = [(0, 1), (1, 0)]

    grads = copies_to_all(output_grads.T, "y").reshape(cores, -1, output_grads.shape[0])
    product = (
        jax.ShapeDtypeStruct((grads.shape[1], activations.shape[1]), BF16),
        jax.ShapeDtypeStruct((8, LANES), F32),
    )
    value, top = pl.pallas_call(
        multiply_for_other,
        out_shape=product,
        in_specs=[SMEM, VMEM, VMEM],
        out_specs=(VMEM, VMEM),
        compiler_params=PARAMS,
    )(core, grads, activations)

    value = lax.ppermute(value, "core", swap)
    value, top = pl.pallas_call(
        multiply_and_add,
        out_shape=product,
        in_specs=[SMEM] + [VMEM] * 4,
        out_specs=(VMEM, VMEM),
        compiler_params=PARAMS,
    )(core, grads, activations, value, top)
    value = lax.all_to_all(value.reshape(xs, rows, -1), "x", 0, 0, tiled=True)
    value = pl.pallas_call(
        add_and_cut,
        out_shape=jax.ShapeDtypeStruct((zs, packed, LANES), BF16),
        in_specs=[VMEM],
        out_specs=VMEM,
    )(value)
    value = lax.all_to_all(value, "z", 0, 0, tiled=True)
    value = jnp.sum(value.astype(F32), axis=0)
    route = []
    for x in range(xs):
        for z in range(zs):
            for half in range(cores):
                for y in range(ys):
                    source = ((x * zs + z) * cores + half) * ys + y
                    route.append((source, (y * zs + z) * ys + half * xs + x))
    value = lax.ppermute(value, DEVICE, route)

    block = jax.ShapeDtypeStruct((rows, width), F32)
    master_new, second_new, moment, held = pl.pallas_call(
        functools.partial(adam_step, xs * zs * cores),
        out_shape=(block, block, block, jax.ShapeDtypeStruct((zs, sent_rows, LANES), BF16)),
        in_specs=[SMEM, SMEM] + [VMEM] * 5,
        out_specs=(VMEM,) * 4,
    )(core, moment_range, value, top, master, moment_q, second_moment)

    held = lax.all_to_all(held, "z", 0, 0, tiled=True)
    held = copies_to_all(held, "x").reshape(xs, zs, sent_rows, LANES)
    other = lax.ppermute(held, "core", swap)
    tops = pl.pallas_call(
        join_tops,
        out_shape=jax.ShapeDtypeStruct((cores * ys, 8, LANES), F32),
        in_specs=[VMEM],
        out_specs=VMEM,
    )(held)
    tops = lax.all_to_all(tops, ("core", "y"), 0, 0, tiled=True)

    one = jax.ShapeDtypeStruct((1,), F32)
    weight_q, moment_q_new, moment_span, weight_span, grad_span = pl.pallas_call(
        scale_weights,
        grid=(xs,),
        out_shape=(
            jax.ShapeDtypeStruct((rows, width * xs * zs * cores), BF16),
            jax.ShapeDtypeStruct((rows, width), BF16),
            one,
            one,
            one,
        ),
        in_specs=[SMEM, VMEM, VMEM, VMEM, VMEM],
        out_specs=(
            pl.BlockSpec((rows, width * zs * cores), lambda i: (0, i)),
            VMEM,
            SMEM,
            SMEM,
            SMEM,
        ),
        scratch_shapes=[pltpu.VMEM((8, LANES), F32)],
        compiler_params=pltpu.CompilerParams(vmem_limit_bytes=8 * 1024 * 1024),
    )(core, tops, held, other, moment)
    return master_new, moment_q_new, moment_span, second_new, weight_q, weight_span, grad_span


def solution(mesh):
    inner = Mesh(mesh.devices.reshape(4, 8, 2, 8), DEVICE)
    dp, mp = ("x", "z", "core"), "y"
    placed = (P(dp, mp), P(dp, mp), P(mp, dp), P(mp, dp), P(), P(mp, dp))
    return jax.shard_map(
        on_device,
        mesh=inner,
        in_specs=placed,
        out_specs=(P(mp, dp), P(mp, dp), P(), P(mp, dp), P(mp, None), P(), P()),
        check_vma=False,
    )
```

```python
import functools

import jax
import jax.numpy as jnp
from jax import lax
from jax.experimental import pallas as pl
from jax.experimental.pallas import tpu as pltpu
from jax.sharding import Mesh, PartitionSpec as P

EPSILON = 1e-06
BETA_ONE = 0.9
BETA_TWO = 0.999
LEARN_RATE = 0.001
DECAY_RATE = 0.1
ADAM_EPSILON = 1e-08

F32 = jnp.float32
BF16 = jnp.bfloat16
LANES = 128
HALF = LANES // 2
TOP_ROWS = 16
TILE = 512
DEVICE = ("x", "z", "core", "y")
SMEM = pl.BlockSpec(memory_space=pltpu.SMEM)
VMEM = pl.BlockSpec(memory_space=pltpu.VMEM)
MIB = 1024 * 1024


def grant(size):
    return pltpu.CompilerParams(vmem_limit_bytes=size * MIB)


def fold(middle, odd):
    rows = middle.shape[0] // 2
    upper, lower = middle[:rows], pltpu.roll(middle[rows:], HALF, 1)
    left = lax.broadcasted_iota(jnp.int32, upper.shape, 1) < HALF
    return jnp.where(left, lower, upper) if odd else jnp.where(left, upper, lower)


def unfold(even_tail, odd_tail):
    left = lax.broadcasted_iota(jnp.int32, even_tail.shape, 1) < HALF
    upper = jnp.where(left, even_tail, odd_tail)
    lower = pltpu.roll(jnp.where(left, odd_tail, even_tail), HALF, 1)
    return jnp.concatenate([upper, lower], 0)


def largest(value):
    return jnp.max(jnp.max(jnp.abs(value), axis=1, keepdims=True), axis=0, keepdims=True)


def magnitude(value, best):
    top = jnp.max(jnp.abs(value).reshape(-1, 8, value.shape[1]), axis=0)
    for start in range(0, value.shape[1], LANES):
        part = top[:, start : start + LANES]
        best = part if best is None else jnp.maximum(best, part)
    return best


def split(top):
    high = top.astype(BF16).astype(F32)
    middle = (top - high).astype(BF16).astype(F32)
    low = top - high - middle
    row = lax.broadcasted_iota(jnp.int32, top.shape, 0)
    high = jnp.where(row < 4, high, pltpu.roll(low, 4, 0))
    return jnp.concatenate([high, middle], 0).astype(BF16)


def joined(spread):
    spread = spread.astype(F32)
    return spread[:8] + spread[8:] + pltpu.roll(spread[:8], 4, 0)


def copy_grads(grads_ref, out_ref):
    for copy in range(out_ref.shape[0]):
        out_ref[copy] = grads_ref[...]


def multiply_for_other(core_ref, grads_ref, activations_ref, out_ref, top_ref):
    grads = grads_ref[1 - core_ref[0]]
    best = None
    for start in range(0, out_ref.shape[1], TILE):
        where = slice(start, start + TILE)
        value = jnp.dot(grads, activations_ref[:, where], preferred_element_type=F32)
        out_ref[:, where] = value.astype(BF16)
        best = magnitude(value, best)
    top_ref[...] = best


def multiply_and_add(core_ref, grads_ref, activations_ref, other_ref, first_ref, out_ref, top_ref):
    grads = grads_ref[core_ref[0]]
    best = first_ref[...]
    for start in range(0, out_ref.shape[1], TILE):
        where = slice(start, start + TILE)
        value = jnp.dot(grads, activations_ref[:, where], preferred_element_type=F32)
        out_ref[:, where] = (value + other_ref[:, where].astype(F32)).astype(BF16)
        best = magnitude(value, best)
    top_ref[...] = best


def add_and_cut(parts_ref, out_ref):
    rows = parts_ref.shape[1]

    def total(tile):
        where = slice(tile * LANES, (tile + 1) * LANES)
        value = parts_ref[0, :, where].astype(F32)
        for part in range(1, parts_ref.shape[0]):
            value += parts_ref[part, :, where].astype(F32)
        return value

    for pair in range(out_ref.shape[0] // 2):
        middle = total(3 * pair + 1)
        for odd in range(2):
            out_ref[2 * pair + odd, :rows] = total(3 * pair + 2 * odd).astype(BF16)
            out_ref[2 * pair + odd, rows:] = fold(middle, odd).astype(BF16)


def adam_step(
    devices, core_ref, range_ref, summed_ref, top_ref, master_ref, moment_ref, second_ref,
    master_out, second_out, moment_out, sent_out,
):
    rows = master_ref.shape[0]
    is_even = core_ref[0] == 0
    own, tail = summed_ref[:rows], summed_ref[rows:]
    middle = unfold(tail, tail)
    gradient = jnp.where(
        is_even,
        jnp.concatenate([own, middle[:, :HALF]], 1),
        jnp.concatenate([middle[:, HALF:], own], 1),
    ) / devices
    moment = (
        BETA_ONE * (moment_ref[...].astype(F32) * range_ref[0]) + (1.0 - BETA_ONE) * gradient
    )
    second_new = BETA_TWO * second_ref[...] + (1.0 - BETA_TWO) * gradient * gradient
    master = master_ref[...]
    master_new = master - LEARN_RATE * (
        moment / (jnp.sqrt(second_new) + ADAM_EPSILON) + DECAY_RATE * master
    )
    master_out[...] = master_new
    second_out[...] = second_new
    moment_out[...] = moment
    own = jnp.where(is_even, master_new[:, :LANES], master_new[:, HALF:]).astype(BF16)
    middle = jnp.concatenate([master_new[:, LANES:], master_new[:, :HALF]], 1)
    tail = jnp.where(is_even, fold(middle, False), fold(middle, True)).astype(BF16)
    row = lax.broadcasted_iota(jnp.int32, (8, LANES), 0)
    tops = (largest(top_ref[...]), largest(moment), largest(master_new))
    spread = split(jnp.where(row == 0, tops[0], jnp.where(row == 1, tops[1], tops[2])))
    for copy in range(sent_out.shape[0]):
        sent_out[copy, :rows] = own
        sent_out[copy, rows : rows + rows // 2] = tail
        sent_out[copy, rows + rows // 2 :] = spread


def join_blocks(held_ref, out_ref):
    packed = held_ref.shape[1] - TOP_ROWS
    best = None
    for z in range(held_ref.shape[0]):
        out_ref[z * packed : (z + 1) * packed] = held_ref[z, :packed]
        top = joined(held_ref[z, packed:])
        best = top if best is None else jnp.maximum(best, top)
    out_ref[held_ref.shape[0] * packed :] = split(best)


def join_tops(held_ref, out_ref):
    packed = held_ref.shape[1] - TOP_ROWS
    best = joined(held_ref[0, packed:])
    for x in range(1, held_ref.shape[0]):
        best = jnp.maximum(best, joined(held_ref[x, packed:]))
    for copy in range(out_ref.shape[0]):
        out_ref[copy] = best


def scale_weights(
    core_ref, tops_ref, own_ref, other_ref, moment_ref,
    weight_out, moment_out, moment_span_out, weight_span_out, grad_span_out, span_ref,
):
    rows = weight_out.shape[0]
    packed = rows + rows // 2
    step = pl.program_id(0)
    is_even = core_ref[0] == 0

    @pl.when(step == 0)
    def _():
        best = tops_ref[0]
        for place in range(1, tops_ref.shape[0]):
            best = jnp.maximum(best, tops_ref[place])
        spans = best + EPSILON
        span_ref[...] = spans
        moment_out[...] = (moment_ref[...] / largest(spans[1:2])).astype(BF16)
        grad_span_out[0] = jnp.max(spans[0:1])
        moment_span_out[0] = jnp.max(spans[1:2])
        weight_span_out[0] = jnp.max(spans[2:3])

    span = span_ref[2:3]
    for place in range((own_ref.shape[1] - TOP_ROWS) // packed):
        where = slice(place * packed, (place + 1) * packed)
        own = own_ref[step, where].astype(F32) / span
        other = other_ref[step, where].astype(F32) / span
        even, odd = jnp.where(is_even, own, other), jnp.where(is_even, other, own)
        start = 3 * LANES * place
        weight_out[:, start : start + LANES] = even[:rows].astype(BF16)
        weight_out[:, start + LANES : start + 2 * LANES] = unfold(even[rows:], odd[rows:]).astype(BF16)
        weight_out[:, start + 2 * LANES : start + 3 * LANES] = odd[:rows].astype(BF16)


def on_device(activations, output_grads, master, moment_q, moment_range, second_moment):
    xs, zs, cores, ys = (lax.axis_size(name) for name in DEVICE)
    rows, width = master.shape
    packed = rows + rows // 2
    sent_rows = packed + TOP_ROWS
    core = lax.axis_index("core").reshape(1)
    output_grads, core = lax.optimization_barrier((output_grads, core))
    swap = [(0, 1), (1, 0)]

    tokens, columns = output_grads.shape
    grads = pl.pallas_call(
        copy_grads,
        out_shape=jax.ShapeDtypeStruct((ys, columns, tokens), BF16),
        in_specs=[VMEM],
        out_specs=VMEM,
        compiler_params=grant(4),
    )(output_grads.T)
    grads = lax.all_to_all(grads, "y", 0, 0, tiled=True).reshape(cores, -1, tokens)
    product = (
        jax.ShapeDtypeStruct((grads.shape[1], activations.shape[1]), BF16),
        jax.ShapeDtypeStruct((8, LANES), F32),
    )
    value, top = pl.pallas_call(
        multiply_for_other,
        out_shape=product,
        in_specs=[SMEM, VMEM, VMEM],
        out_specs=(VMEM, VMEM),
        compiler_params=grant(12),
    )(core, grads, activations)

    value = lax.ppermute(value, "core", swap)
    value, top = pl.pallas_call(
        multiply_and_add,
        out_shape=product,
        in_specs=[SMEM] + [VMEM] * 4,
        out_specs=(VMEM, VMEM),
        compiler_params=grant(12),
    )(core, grads, activations, value, top)
    value = lax.all_to_all(value.reshape(xs, rows, -1), "x", 0, 0, tiled=True)
    value = pl.pallas_call(
        add_and_cut,
        out_shape=jax.ShapeDtypeStruct((zs, packed, LANES), BF16),
        in_specs=[VMEM],
        out_specs=VMEM,
        compiler_params=grant(4),
    )(value)
    value = lax.all_to_all(value, "z", 0, 0, tiled=True)
    value = jnp.sum(value.astype(F32), axis=0)
    route = []
    for x in range(xs):
        for z in range(zs):
            for half in range(cores):
                for y in range(ys):
                    source = ((x * zs + z) * cores + half) * ys + y
                    route.append((source, (y * zs + z) * ys + half * xs + x))
    value = lax.ppermute(value, DEVICE, route)

    block = jax.ShapeDtypeStruct((rows, width), F32)
    master_new, second_new, moment, held = pl.pallas_call(
        functools.partial(adam_step, xs * zs * cores),
        out_shape=(block, block, block, jax.ShapeDtypeStruct((zs, sent_rows, LANES), BF16)),
        in_specs=[SMEM, SMEM] + [VMEM] * 5,
        out_specs=(VMEM,) * 4,
        compiler_params=grant(4),
    )(core, moment_range, value, top, master, moment_q, second_moment)

    held = lax.all_to_all(held, "z", 0, 0, tiled=True)
    held = pl.pallas_call(
        join_blocks,
        out_shape=jax.ShapeDtypeStruct((zs * packed + TOP_ROWS, LANES), BF16),
        in_specs=[VMEM],
        out_specs=VMEM,
        compiler_params=grant(4),
    )(held)
    held = lax.all_gather(held, "x")
    other = lax.ppermute(held, "core", swap)
    tops = pl.pallas_call(
        join_tops,
        out_shape=jax.ShapeDtypeStruct((cores * ys, 8, LANES), F32),
        in_specs=[VMEM],
        out_specs=VMEM,
        compiler_params=grant(4),
    )(held)
    tops = lax.all_to_all(tops, ("core", "y"), 0, 0, tiled=True)

    one = jax.ShapeDtypeStruct((1,), F32)
    weight_q, moment_q_new, moment_span, weight_span, grad_span = pl.pallas_call(
        scale_weights,
        grid=(xs,),
        out_shape=(
            jax.ShapeDtypeStruct((rows, width * xs * zs * cores), BF16),
            jax.ShapeDtypeStruct((rows, width), BF16),
            one,
            one,
            one,
        ),
        in_specs=[SMEM, VMEM, VMEM, VMEM, VMEM],
        out_specs=(
            pl.BlockSpec((rows, width * zs * cores), lambda i: (0, i)),
            VMEM,
            SMEM,
            SMEM,
            SMEM,
        ),
        scratch_shapes=[pltpu.VMEM((8, LANES), F32)],
        compiler_params=grant(8),
    )(core, tops, held, other, moment)
    return master_new, moment_q_new, moment_span, second_new, weight_q, weight_span, grad_span


def solution(mesh):
    inner = Mesh(mesh.devices.reshape(4, 8, 2, 8), DEVICE)
    dp, mp = ("x", "z", "core"), "y"
    placed = (P(dp, mp), P(dp, mp), P(mp, dp), P(mp, dp), P(), P(mp, dp))
    return jax.shard_map(
        on_device,
        mesh=inner,
        in_specs=placed,
        out_specs=(P(mp, dp), P(mp, dp), P(), P(mp, dp), P(mp, None), P(), P()),
        check_vma=False,
    )
```

```python
import functools

import jax
import jax.numpy as jnp
from jax import lax
from jax.experimental import pallas as pl
from jax.experimental.pallas import tpu as pltpu
from jax.sharding import Mesh, PartitionSpec as P

EPSILON = 1e-06
BETA_ONE = 0.9
BETA_TWO = 0.999
LEARN_RATE = 0.001
DECAY_RATE = 0.1
ADAM_EPSILON = 1e-08

F32 = jnp.float32
BF16 = jnp.bfloat16
LANES = 128
HALF = LANES // 2
TOP_ROWS = 16
TILE = 512
DEVICE = ("x", "z", "core", "y")
SMEM = pl.BlockSpec(memory_space=pltpu.SMEM)
VMEM = pl.BlockSpec(memory_space=pltpu.VMEM)
MIB = 1024 * 1024


def grant(size):
    return pltpu.CompilerParams(vmem_limit_bytes=size * MIB)


def fold(middle, odd):
    rows = middle.shape[0] // 2
    upper, lower = middle[:rows], pltpu.roll(middle[rows:], HALF, 1)
    left = lax.broadcasted_iota(jnp.int32, upper.shape, 1) < HALF
    return jnp.where(left, lower, upper) if odd else jnp.where(left, upper, lower)


def unfold(even_tail, odd_tail):
    left = lax.broadcasted_iota(jnp.int32, even_tail.shape, 1) < HALF
    upper = jnp.where(left, even_tail, odd_tail)
    lower = pltpu.roll(jnp.where(left, odd_tail, even_tail), HALF, 1)
    return jnp.concatenate([upper, lower], 0)


def largest(value):
    return jnp.max(jnp.max(jnp.abs(value), axis=1, keepdims=True), axis=0, keepdims=True)


def magnitude(value, best):
    top = jnp.max(jnp.abs(value).reshape(-1, 8, value.shape[1]), axis=0)
    for start in range(0, value.shape[1], LANES):
        part = top[:, start : start + LANES]
        best = part if best is None else jnp.maximum(best, part)
    return best


def split(top):
    high = top.astype(BF16).astype(F32)
    middle = (top - high).astype(BF16).astype(F32)
    low = top - high - middle
    row = lax.broadcasted_iota(jnp.int32, top.shape, 0)
    high = jnp.where(row < 4, high, pltpu.roll(low, 4, 0))
    return jnp.concatenate([high, middle], 0).astype(BF16)


def joined(spread):
    spread = spread.astype(F32)
    return spread[:8] + spread[8:] + pltpu.roll(spread[:8], 4, 0)


def copy_grads(grads_ref, out_ref):
    for copy in range(out_ref.shape[0]):
        out_ref[copy] = grads_ref[...]


ABOVE = ((4, -1, 0, -2), (-3, 2, 1, 3))


def columns_of(core, x, y):
    place = (x - y // 2) % 4
    if isinstance(y, int):
        return (y + ABOVE[core][place]) % 8
    above = 0
    for half in range(2):
        for step in range(4):
            above = jnp.where((core == half) & (place == step), ABOVE[half][step], above)
    return (y + above + 8) % 8


def slot_of(feature, y):
    near = feature // 2 if feature % 2 == 0 else 7 - feature // 2
    return (near + 4 * (y % 2)) % 8


def core_and_y(place_ref):
    return place_ref[0] // 8, place_ref[0] % 8


def grads_for(core, y, grads_ref):
    return jnp.concatenate([grads_ref[columns_of(core, x, y)] for x in range(4)], 0)


def multiply_for_other(place_ref, grads_ref, activations_ref, out_ref, top_ref):
    core, y = core_and_y(place_ref)
    grads = grads_for(1 - core, y, grads_ref)
    best = None
    for start in range(0, out_ref.shape[1], TILE):
        where = slice(start, start + TILE)
        value = jnp.dot(grads, activations_ref[:, where], preferred_element_type=F32)
        out_ref[:, where] = value.astype(BF16)
        best = magnitude(value, best)
    top_ref[...] = best


def multiply_and_add(place_ref, grads_ref, activations_ref, other_ref, first_ref, out_ref, top_ref):
    grads = grads_for(*core_and_y(place_ref), grads_ref)
    best = first_ref[...]
    for start in range(0, out_ref.shape[1], TILE):
        where = slice(start, start + TILE)
        value = jnp.dot(grads, activations_ref[:, where], preferred_element_type=F32)
        out_ref[:, where] = (value + other_ref[:, where].astype(F32)).astype(BF16)
        best = magnitude(value, best)
    top_ref[...] = best


def add_and_cut(place_ref, parts_ref, out_ref):
    y = core_and_y(place_ref)[1]
    rows = parts_ref.shape[1]

    def total(tile):
        where = slice(tile * LANES, (tile + 1) * LANES)
        value = parts_ref[0, :, where].astype(F32)
        for part in range(1, parts_ref.shape[0]):
            value += parts_ref[part, :, where].astype(F32)
        return value

    for pair in range(out_ref.shape[0] // 2):
        middle = total(3 * pair + 1)
        for odd in range(2):
            slot = slot_of(2 * pair + odd, y)
            out_ref[slot, :rows] = total(3 * pair + 2 * odd).astype(BF16)
            out_ref[slot, rows:] = fold(middle, odd).astype(BF16)


def adam_step(
    devices, place_ref, range_ref, summed_ref, top_ref, master_ref, moment_ref, second_ref,
    master_out, second_out, moment_out, sent_out,
):
    rows = master_ref.shape[0]
    is_even = core_and_y(place_ref)[0] == 0
    own, tail = summed_ref[:rows], summed_ref[rows:]
    middle = unfold(tail, tail)
    gradient = jnp.where(
        is_even,
        jnp.concatenate([own, middle[:, :HALF]], 1),
        jnp.concatenate([middle[:, HALF:], own], 1),
    ) / devices
    moment = (
        BETA_ONE * (moment_ref[...].astype(F32) * range_ref[0]) + (1.0 - BETA_ONE) * gradient
    )
    second_new = BETA_TWO * second_ref[...] + (1.0 - BETA_TWO) * gradient * gradient
    master = master_ref[...]
    master_new = master - LEARN_RATE * (
        moment / (jnp.sqrt(second_new) + ADAM_EPSILON) + DECAY_RATE * master
    )
    master_out[...] = master_new
    second_out[...] = second_new
    moment_out[...] = moment
    own = jnp.where(is_even, master_new[:, :LANES], master_new[:, HALF:]).astype(BF16)
    middle = jnp.concatenate([master_new[:, LANES:], master_new[:, :HALF]], 1)
    tail = jnp.where(is_even, fold(middle, False), fold(middle, True)).astype(BF16)
    row = lax.broadcasted_iota(jnp.int32, (8, LANES), 0)
    tops = (largest(top_ref[...]), largest(moment), largest(master_new))
    spread = split(jnp.where(row == 0, tops[0], jnp.where(row == 1, tops[1], tops[2])))
    for copy in range(sent_out.shape[0]):
        sent_out[copy, :rows] = own
        sent_out[copy, rows : rows + rows // 2] = tail
        sent_out[copy, rows + rows // 2 :] = spread


def join_blocks(held_ref, out_ref):
    packed = held_ref.shape[1] - TOP_ROWS
    best = None
    for z in range(held_ref.shape[0]):
        out_ref[z * packed : (z + 1) * packed] = held_ref[z, :packed]
        top = joined(held_ref[z, packed:])
        best = top if best is None else jnp.maximum(best, top)
    out_ref[held_ref.shape[0] * packed :] = split(best)


def join_tops(held_ref, out_ref):
    packed = held_ref.shape[1] - TOP_ROWS
    best = joined(held_ref[0, packed:])
    for x in range(1, held_ref.shape[0]):
        best = jnp.maximum(best, joined(held_ref[x, packed:]))
    for copy in range(out_ref.shape[0]):
        out_ref[copy] = best


def scale_weights(
    place_ref, tops_ref, own_ref, other_ref, moment_ref,
    weight_out, moment_out, moment_span_out, weight_span_out, grad_span_out, span_ref,
):
    rows = weight_out.shape[0]
    packed = rows + rows // 2
    step = pl.program_id(0)
    is_even = core_and_y(place_ref)[0] == 0

    @pl.when(step == 0)
    def _():
        best = tops_ref[0]
        for place in range(1, tops_ref.shape[0]):
            best = jnp.maximum(best, tops_ref[place])
        spans = best + EPSILON
        span_ref[...] = spans
        moment_out[...] = (moment_ref[...] / largest(spans[1:2])).astype(BF16)
        grad_span_out[0] = jnp.max(spans[0:1])
        moment_span_out[0] = jnp.max(spans[1:2])
        weight_span_out[0] = jnp.max(spans[2:3])

    scale = 1.0 / span_ref[2:3]
    for place in range((own_ref.shape[1] - TOP_ROWS) // packed):
        where = slice(place * packed, (place + 1) * packed)
        own = own_ref[step, where].astype(F32) * scale
        other = other_ref[step, where].astype(F32) * scale
        even, odd = jnp.where(is_even, own, other), jnp.where(is_even, other, own)
        start = 3 * LANES * place
        weight_out[:, start : start + LANES] = even[:rows].astype(BF16)
        weight_out[:, start + LANES : start + 2 * LANES] = unfold(even[rows:], odd[rows:]).astype(BF16)
        weight_out[:, start + 2 * LANES : start + 3 * LANES] = odd[:rows].astype(BF16)


def on_device(activations, output_grads, master, moment_q, moment_range, second_moment):
    xs, zs, cores, ys = (lax.axis_size(name) for name in DEVICE)
    rows, width = master.shape
    packed = rows + rows // 2
    sent_rows = packed + TOP_ROWS
    place = lax.axis_index(("core", "y")).reshape(1)
    output_grads, place = lax.optimization_barrier((output_grads, place))
    swap = [(0, 1), (1, 0)]

    tokens, columns = output_grads.shape
    grads = pl.pallas_call(
        copy_grads,
        out_shape=jax.ShapeDtypeStruct((ys, columns, tokens), BF16),
        in_specs=[VMEM],
        out_specs=VMEM,
        compiler_params=grant(4),
    )(output_grads.T)
    grads = lax.all_to_all(grads, "y", 0, 0, tiled=True)
    product = (
        jax.ShapeDtypeStruct((xs * columns, activations.shape[1]), BF16),
        jax.ShapeDtypeStruct((8, LANES), F32),
    )
    value, top = pl.pallas_call(
        multiply_for_other,
        out_shape=product,
        in_specs=[SMEM, VMEM, VMEM],
        out_specs=(VMEM, VMEM),
        compiler_params=grant(12),
    )(place, grads, activations)

    value = lax.ppermute(value, "core", swap)
    value, top = pl.pallas_call(
        multiply_and_add,
        out_shape=product,
        in_specs=[SMEM] + [VMEM] * 4,
        out_specs=(VMEM, VMEM),
        compiler_params=grant(12),
    )(place, grads, activations, value, top)
    value = lax.all_to_all(value.reshape(xs, rows, -1), "x", 0, 0, tiled=True)
    value = pl.pallas_call(
        add_and_cut,
        out_shape=jax.ShapeDtypeStruct((zs, packed, LANES), BF16),
        in_specs=[SMEM, VMEM],
        out_specs=VMEM,
        compiler_params=grant(4),
    )(place, value)
    value = lax.all_to_all(value, "z", 0, 0, tiled=True)
    value = jnp.sum(value.astype(F32), axis=0)
    route = []
    for x in range(xs):
        for half in range(cores):
            for y in range(ys):
                for feature in range(zs):
                    source = ((x * zs + slot_of(feature, y)) * cores + half) * ys + y
                    route.append((source, (y * zs + feature) * ys + columns_of(half, x, y)))
    value = lax.ppermute(value, DEVICE, route)

    block = jax.ShapeDtypeStruct((rows, width), F32)
    master_new, second_new, moment, held = pl.pallas_call(
        functools.partial(adam_step, xs * zs * cores),
        out_shape=(block, block, block, jax.ShapeDtypeStruct((zs, sent_rows, LANES), BF16)),
        in_specs=[SMEM, SMEM] + [VMEM] * 5,
        out_specs=(VMEM,) * 4,
        compiler_params=grant(4),
    )(place, moment_range, value, top, master, moment_q, second_moment)

    held = lax.all_to_all(held, "z", 0, 0, tiled=True)
    held = pl.pallas_call(
        join_blocks,
        out_shape=jax.ShapeDtypeStruct((zs * packed + TOP_ROWS, LANES), BF16),
        in_specs=[VMEM],
        out_specs=VMEM,
        compiler_params=grant(4),
    )(held)
    held = lax.all_gather(held, "x")
    other = lax.ppermute(held, "core", swap)
    tops = pl.pallas_call(
        join_tops,
        out_shape=jax.ShapeDtypeStruct((cores * ys, 8, LANES), F32),
        in_specs=[VMEM],
        out_specs=VMEM,
        compiler_params=grant(4),
    )(held)
    tops = lax.all_to_all(tops, ("core", "y"), 0, 0, tiled=True)

    one = jax.ShapeDtypeStruct((1,), F32)
    weight_q, moment_q_new, moment_span, weight_span, grad_span = pl.pallas_call(
        scale_weights,
        grid=(xs,),
        out_shape=(
            jax.ShapeDtypeStruct((rows, width * xs * zs * cores), BF16),
            jax.ShapeDtypeStruct((rows, width), BF16),
            one,
            one,
            one,
        ),
        in_specs=[SMEM, VMEM, VMEM, VMEM, VMEM],
        out_specs=(
            pl.BlockSpec((rows, width * zs * cores), lambda i: (0, i)),
            VMEM,
            SMEM,
            SMEM,
            SMEM,
        ),
        scratch_shapes=[pltpu.VMEM((8, LANES), F32)],
        compiler_params=grant(8),
    )(place, tops, held, other, moment)
    return master_new, moment_q_new, moment_span, second_new, weight_q, weight_span, grad_span


def solution(mesh):
    inner = Mesh(mesh.devices.reshape(4, 8, 2, 8), DEVICE)
    dp, mp = ("x", "z", "core"), "y"
    placed = (P(dp, mp), P(dp, mp), P(mp, dp), P(mp, dp), P(), P(mp, dp))
    return jax.shard_map(
        on_device,
        mesh=inner,
        in_specs=placed,
        out_specs=(P(mp, dp), P(mp, dp), P(), P(mp, dp), P(mp, None), P(), P()),
        check_vma=False,
    )
```

```python
import functools

import jax
import jax.numpy as jnp
from jax import lax
from jax.experimental import pallas as pl
from jax.experimental.pallas import tpu as pltpu
from jax.sharding import Mesh, PartitionSpec as P

EPSILON = 1e-06
BETA_ONE = 0.9
BETA_TWO = 0.999
LEARN_RATE = 0.001
DECAY_RATE = 0.1
ADAM_EPSILON = 1e-08

F32 = jnp.float32
BF16 = jnp.bfloat16
LANES = 128
HALF = LANES // 2
TOP_ROWS = 16
TILE = 512
DEVICE = ("x", "z", "core", "y")
SMEM = pl.BlockSpec(memory_space=pltpu.SMEM)
VMEM = pl.BlockSpec(memory_space=pltpu.VMEM)
HBM = pl.BlockSpec(memory_space=pltpu.HBM)
MIB = 1024 * 1024


def grant(size):
    return pltpu.CompilerParams(vmem_limit_bytes=size * MIB)


def fold(middle, odd):
    rows = middle.shape[0] // 2
    upper, lower = middle[:rows], pltpu.roll(middle[rows:], HALF, 1)
    left = lax.broadcasted_iota(jnp.int32, upper.shape, 1) < HALF
    return jnp.where(left, lower, upper) if odd else jnp.where(left, upper, lower)


def unfold(even_tail, odd_tail):
    left = lax.broadcasted_iota(jnp.int32, even_tail.shape, 1) < HALF
    upper = jnp.where(left, even_tail, odd_tail)
    lower = pltpu.roll(jnp.where(left, odd_tail, even_tail), HALF, 1)
    return jnp.concatenate([upper, lower], 0)


def largest(value):
    return jnp.max(jnp.max(jnp.abs(value), axis=1, keepdims=True), axis=0, keepdims=True)


def magnitude(value, best):
    top = jnp.max(jnp.abs(value).reshape(-1, 8, value.shape[1]), axis=0)
    for start in range(0, value.shape[1], LANES):
        part = top[:, start : start + LANES]
        best = part if best is None else jnp.maximum(best, part)
    return best


def split(top):
    high = top.astype(BF16).astype(F32)
    middle = (top - high).astype(BF16).astype(F32)
    low = top - high - middle
    row = lax.broadcasted_iota(jnp.int32, top.shape, 0)
    high = jnp.where(row < 4, high, pltpu.roll(low, 4, 0))
    return jnp.concatenate([high, middle], 0).astype(BF16)


def joined(spread):
    spread = spread.astype(F32)
    return spread[:8] + spread[8:] + pltpu.roll(spread[:8], 4, 0)


def copy_grads(grads_ref, out_ref, arrived):
    copies = [
        pltpu.make_async_copy(grads_ref, out_ref.at[copy], arrived.at[copy])
        for copy in range(out_ref.shape[0])
    ]
    for copy in copies:
        copy.start()
    for copy in copies:
        copy.wait()


ABOVE = ((4, -1, 0, -2), (-3, 2, 1, 3))


def columns_of(core, x, y):
    place = (x - y // 2) % 4
    if isinstance(y, int):
        return (y + ABOVE[core][place]) % 8
    above = 0
    for half in range(2):
        for step in range(4):
            above = jnp.where((core == half) & (place == step), ABOVE[half][step], above)
    return (y + above + 8) % 8


def slot_of(feature, y):
    near = feature // 2 if feature % 2 == 0 else 7 - feature // 2
    return (near + 4 * (y % 2)) % 8


def core_and_y(place_ref):
    return place_ref[0] // 8, place_ref[0] % 8


def grads_for(core, y, grads_ref):
    return jnp.concatenate([grads_ref[columns_of(core, x, y)] for x in range(4)], 0)


def multiply_for_other(place_ref, grads_ref, activations_ref, out_ref, top_ref):
    core, y = core_and_y(place_ref)
    grads = grads_for(1 - core, y, grads_ref)
    best = None
    for start in range(0, out_ref.shape[1], TILE):
        where = slice(start, start + TILE)
        value = jnp.dot(grads, activations_ref[:, where], preferred_element_type=F32)
        out_ref[:, where] = value.astype(BF16)
        best = magnitude(value, best)
    top_ref[...] = best


def multiply_and_add(place_ref, grads_ref, activations_ref, other_ref, first_ref, out_ref, top_ref):
    grads = grads_for(*core_and_y(place_ref), grads_ref)
    best = first_ref[...]
    for start in range(0, out_ref.shape[1], TILE):
        where = slice(start, start + TILE)
        value = jnp.dot(grads, activations_ref[:, where], preferred_element_type=F32)
        out_ref[:, where] = (value + other_ref[:, where].astype(F32)).astype(BF16)
        best = magnitude(value, best)
    top_ref[...] = best


def add_and_cut(place_ref, parts_ref, out_ref):
    y = core_and_y(place_ref)[1]
    rows = parts_ref.shape[1]

    def total(tile):
        where = slice(tile * LANES, (tile + 1) * LANES)
        value = parts_ref[0, :, where].astype(F32)
        for part in range(1, parts_ref.shape[0]):
            value += parts_ref[part, :, where].astype(F32)
        return value

    for pair in range(out_ref.shape[0] // 2):
        middle = total(3 * pair + 1)
        for odd in range(2):
            slot = slot_of(2 * pair + odd, y)
            out_ref[slot, :rows] = total(3 * pair + 2 * odd).astype(BF16)
            out_ref[slot, rows:] = fold(middle, odd).astype(BF16)


def step_of(gradient, moment, second_moment, master):
    moment = BETA_ONE * moment + (1.0 - BETA_ONE) * gradient
    second_new = BETA_TWO * second_moment + (1.0 - BETA_TWO) * gradient * gradient
    master_new = master - LEARN_RATE * (
        moment / (jnp.sqrt(second_new) + ADAM_EPSILON) + DECAY_RATE * master
    )
    return moment, second_new, master_new


def pack(value, is_even):
    own = jnp.where(is_even, value[:, :LANES], value[:, HALF:])
    middle = jnp.concatenate([value[:, LANES:], value[:, :HALF]], 1)
    return own, jnp.where(is_even, fold(middle, False), fold(middle, True))


def pack_state(place_ref, range_ref, moment_ref, second_ref, master_ref, out_ref):
    is_even = core_and_y(place_ref)[0] == 0
    rows = master_ref.shape[0]
    moment = moment_ref[...].astype(F32) * range_ref[0]
    for place, state in enumerate((moment, second_ref[...], master_ref[...])):
        own, tail = pack(state, is_even)
        out_ref[place, :rows] = own
        out_ref[place, rows:] = tail


def add_and_find_tops(devices, parts_ref, state_ref, top_ref, sum_out, tops_out):
    total = parts_ref[0].astype(F32)
    for part in range(1, parts_ref.shape[0]):
        total += parts_ref[part].astype(F32)
    sum_out[...] = total
    moment, _, master_new = step_of(total / devices, state_ref[0], state_ref[1], state_ref[2])
    row = lax.broadcasted_iota(jnp.int32, (8, LANES), 0)
    tops = (largest(top_ref[...]), largest(moment), largest(master_new))
    tops = jnp.where(row == 0, tops[0], jnp.where(row == 1, tops[1], tops[2]))
    for copy in range(tops_out.shape[0]):
        tops_out[copy] = tops


def adam_step(
    devices, place_ref, range_ref, summed_ref, tops_ref, moment_ref, second_ref, master_ref,
    master_out, second_out, moment_out, sent_out,
):
    rows = master_ref.shape[0]
    is_even = core_and_y(place_ref)[0] == 0
    own, tail = summed_ref[:rows], summed_ref[rows:]
    middle = unfold(tail, tail)
    gradient = jnp.where(
        is_even,
        jnp.concatenate([own, middle[:, :HALF]], 1),
        jnp.concatenate([middle[:, HALF:], own], 1),
    ) / devices
    moment_out[...], second_out[...], master_new = step_of(
        gradient, moment_ref[...].astype(F32) * range_ref[0], second_ref[...], master_ref[...]
    )
    master_out[...] = master_new
    own, tail = pack(master_new, is_even)
    top = tops_ref[0]
    for place in range(1, tops_ref.shape[0]):
        top = jnp.maximum(top, tops_ref[place])
    spread = split(top)
    for copy in range(sent_out.shape[0]):
        sent_out[copy, :rows] = own.astype(BF16)
        sent_out[copy, rows : rows + rows // 2] = tail.astype(BF16)
        sent_out[copy, rows + rows // 2 :] = spread


def join_blocks(held_ref, out_ref):
    packed = held_ref.shape[1] - TOP_ROWS
    best = None
    for z in range(held_ref.shape[0]):
        out_ref[z * packed : (z + 1) * packed] = held_ref[z, :packed]
        top = joined(held_ref[z, packed:])
        best = top if best is None else jnp.maximum(best, top)
    out_ref[held_ref.shape[0] * packed :] = split(best)


def scale_weights(
    place_ref, own_ref, other_ref, moment_ref,
    weight_out, moment_out, moment_span_out, weight_span_out, grad_span_out, span_ref,
):
    rows = weight_out.shape[0]
    packed = rows + rows // 2
    step = pl.program_id(0)
    is_even = core_and_y(place_ref)[0] == 0

    @pl.when(step == 0)
    def _():
        best = jnp.zeros((8, LANES), F32)
        for held_ref in (own_ref, other_ref):
            for x in range(held_ref.shape[0]):
                best = jnp.maximum(best, joined(held_ref[x, held_ref.shape[1] - TOP_ROWS :]))
        spans = best + EPSILON
        span_ref[...] = spans
        moment_out[...] = (moment_ref[...] / largest(spans[1:2])).astype(BF16)
        grad_span_out[0] = jnp.max(spans[0:1])
        moment_span_out[0] = jnp.max(spans[1:2])
        weight_span_out[0] = jnp.max(spans[2:3])

    scale = 1.0 / span_ref[2:3]
    for place in range((own_ref.shape[1] - TOP_ROWS) // packed):
        where = slice(place * packed, (place + 1) * packed)
        own = own_ref[step, where].astype(F32) * scale
        other = other_ref[step, where].astype(F32) * scale
        even, odd = jnp.where(is_even, own, other), jnp.where(is_even, other, own)
        start = 3 * LANES * place
        weight_out[:, start : start + LANES] = even[:rows].astype(BF16)
        weight_out[:, start + LANES : start + 2 * LANES] = unfold(even[rows:], odd[rows:]).astype(BF16)
        weight_out[:, start + 2 * LANES : start + 3 * LANES] = odd[:rows].astype(BF16)


def on_device(activations, output_grads, master, moment_q, moment_range, second_moment):
    xs, zs, cores, ys = (lax.axis_size(name) for name in DEVICE)
    rows, width = master.shape
    packed = rows + rows // 2
    sent_rows = packed + TOP_ROWS
    place = lax.axis_index(("core", "y")).reshape(1)
    output_grads, place = lax.optimization_barrier((output_grads, place))
    swap = [(0, 1), (1, 0)]

    route = []
    for x in range(xs):
        for half in range(cores):
            for y in range(ys):
                for feature in range(zs):
                    source = ((x * zs + slot_of(feature, y)) * cores + half) * ys + y
                    route.append((source, (y * zs + feature) * ys + columns_of(half, x, y)))
    state = pl.pallas_call(
        pack_state,
        out_shape=jax.ShapeDtypeStruct((3, packed, LANES), F32),
        in_specs=[SMEM, SMEM] + [VMEM] * 3,
        out_specs=VMEM,
        compiler_params=grant(4),
    )(place, moment_range, moment_q, second_moment, master)
    state = lax.ppermute(state, DEVICE, [(owner, source) for source, owner in route])

    tokens, columns = output_grads.shape
    grads = pl.pallas_call(
        copy_grads,
        out_shape=jax.ShapeDtypeStruct((ys, columns, tokens), BF16),
        in_specs=[HBM],
        out_specs=HBM,
        scratch_shapes=[pltpu.SemaphoreType.DMA((ys,))],
        compiler_params=grant(60),
    )(output_grads.T)
    grads = lax.all_to_all(grads, "y", 0, 0, tiled=True)
    grads, state = lax.optimization_barrier((grads, state))
    product = (
        jax.ShapeDtypeStruct((xs * columns, activations.shape[1]), BF16),
        jax.ShapeDtypeStruct((8, LANES), F32),
    )
    value, top = pl.pallas_call(
        multiply_for_other,
        out_shape=product,
        in_specs=[SMEM, VMEM, VMEM],
        out_specs=(VMEM, VMEM),
        compiler_params=grant(12),
    )(place, grads, activations)

    value = lax.ppermute(value, "core", swap)
    value, top = pl.pallas_call(
        multiply_and_add,
        out_shape=product,
        in_specs=[SMEM] + [VMEM] * 4,
        out_specs=(VMEM, VMEM),
        compiler_params=grant(12),
    )(place, grads, activations, value, top)
    value = lax.all_to_all(value.reshape(xs, rows, -1), "x", 0, 0, tiled=True)
    value = pl.pallas_call(
        add_and_cut,
        out_shape=jax.ShapeDtypeStruct((zs, packed, LANES), BF16),
        in_specs=[SMEM, VMEM],
        out_specs=VMEM,
        compiler_params=grant(4),
    )(place, value)
    value = lax.all_to_all(value, "z", 0, 0, tiled=True)
    value, tops = pl.pallas_call(
        functools.partial(add_and_find_tops, xs * zs * cores),
        out_shape=(
            jax.ShapeDtypeStruct((packed, LANES), F32),
            jax.ShapeDtypeStruct((ys, 8, LANES), F32),
        ),
        in_specs=[VMEM] * 3,
        out_specs=(VMEM, VMEM),
        compiler_params=grant(4),
    )(value, state, top)

    value = lax.ppermute(value, DEVICE, route)
    tops = lax.all_to_all(tops, "y", 0, 0, tiled=True)
    block = jax.ShapeDtypeStruct((rows, width), F32)
    master_new, second_new, moment, held = pl.pallas_call(
        functools.partial(adam_step, xs * zs * cores),
        out_shape=(block, block, block, jax.ShapeDtypeStruct((zs, sent_rows, LANES), BF16)),
        in_specs=[SMEM, SMEM] + [VMEM] * 5,
        out_specs=(VMEM,) * 4,
        compiler_params=grant(4),
    )(place, moment_range, value, tops, moment_q, second_moment, master)

    held = lax.all_to_all(held, "z", 0, 0, tiled=True)
    held = pl.pallas_call(
        join_blocks,
        out_shape=jax.ShapeDtypeStruct((zs * packed + TOP_ROWS, LANES), BF16),
        in_specs=[VMEM],
        out_specs=VMEM,
        compiler_params=grant(4),
    )(held)
    held = lax.all_gather(held, "x")
    other = lax.ppermute(held, "core", swap)
    one = jax.ShapeDtypeStruct((1,), F32)
    weight_q, moment_q_new, moment_span, weight_span, grad_span = pl.pallas_call(
        scale_weights,
        grid=(xs,),
        out_shape=(
            jax.ShapeDtypeStruct((rows, width * xs * zs * cores), BF16),
            jax.ShapeDtypeStruct((rows, width), BF16),
            one,
            one,
            one,
        ),
        in_specs=[SMEM, VMEM, VMEM, VMEM],
        out_specs=(
            pl.BlockSpec((rows, width * zs * cores), lambda i: (0, i)),
            VMEM,
            SMEM,
            SMEM,
            SMEM,
        ),
        scratch_shapes=[pltpu.VMEM((8, LANES), F32)],
        compiler_params=grant(8),
    )(place, held, other, moment)
    return master_new, moment_q_new, moment_span, second_new, weight_q, weight_span, grad_span


def solution(mesh):
    inner = Mesh(mesh.devices.reshape(4, 8, 2, 8), DEVICE)
    dp, mp = ("x", "z", "core"), "y"
    placed = (P(dp, mp), P(dp, mp), P(mp, dp), P(mp, dp), P(), P(mp, dp))
    return jax.shard_map(
        on_device,
        mesh=inner,
        in_specs=placed,
        out_specs=(P(mp, dp), P(mp, dp), P(), P(mp, dp), P(mp, None), P(), P()),
        check_vma=False,
    )
```

```python
import functools

import jax
import jax.numpy as jnp
from jax import lax
from jax.experimental import pallas as pl
from jax.experimental.pallas import tpu as pltpu
from jax.sharding import Mesh, PartitionSpec as P

EPSILON = 1e-06
BETA_ONE = 0.9
BETA_TWO = 0.999
LEARN_RATE = 0.001
DECAY_RATE = 0.1
ADAM_EPSILON = 1e-08

F32 = jnp.float32
BF16 = jnp.bfloat16
LANES = 128
HALF = LANES // 2
TOP_ROWS = 16
TILE = 512
DEVICE = ("x", "z", "core", "y")
SMEM = pl.BlockSpec(memory_space=pltpu.SMEM)
VMEM = pl.BlockSpec(memory_space=pltpu.VMEM)
MIB = 1024 * 1024


def grant(size):
    return pltpu.CompilerParams(vmem_limit_bytes=size * MIB)


def fold(middle, odd):
    rows = middle.shape[0] // 2
    upper, lower = middle[:rows], pltpu.roll(middle[rows:], HALF, 1)
    left = lax.broadcasted_iota(jnp.int32, upper.shape, 1) < HALF
    return jnp.where(left, lower, upper) if odd else jnp.where(left, upper, lower)


def unfold(even_tail, odd_tail):
    left = lax.broadcasted_iota(jnp.int32, even_tail.shape, 1) < HALF
    upper = jnp.where(left, even_tail, odd_tail)
    lower = pltpu.roll(jnp.where(left, odd_tail, even_tail), HALF, 1)
    return jnp.concatenate([upper, lower], 0)


def largest(value):
    return jnp.max(jnp.max(jnp.abs(value), axis=1, keepdims=True), axis=0, keepdims=True)


def magnitude(value, best):
    top = jnp.max(jnp.abs(value).reshape(-1, 8, value.shape[1]), axis=0)
    for start in range(0, value.shape[1], LANES):
        part = top[:, start : start + LANES]
        best = part if best is None else jnp.maximum(best, part)
    return best


def split(top):
    high = top.astype(BF16).astype(F32)
    middle = (top - high).astype(BF16).astype(F32)
    low = top - high - middle
    row = lax.broadcasted_iota(jnp.int32, top.shape, 0)
    high = jnp.where(row < 4, high, pltpu.roll(low, 4, 0))
    return jnp.concatenate([high, middle], 0).astype(BF16)


def joined(spread):
    spread = spread.astype(F32)
    return spread[:8] + spread[8:] + pltpu.roll(spread[:8], 4, 0)


ABOVE = (((4, 0), (-1, 3)), ((2, -2), (-3, 1)))


def block_of(core, odd, which, y):
    place = (core + odd) % 2 + 2 * which
    if isinstance(core, int):
        above = ABOVE[core][odd][which]
    else:
        above = jnp.where(core == 0, ABOVE[0][odd][which], ABOVE[1][odd][which])
    return (place + y // 2) % 4, (y + above + 8) % 8


def slot_of(feature, y):
    near = feature // 2 if feature % 2 == 0 else 7 - feature // 2
    return (near + 4 * (y % 2)) % 8


def core_and_y(place_ref):
    return place_ref[0] // 8, place_ref[0] % 8


def multiply(grads, activations_ref, best, *outs):
    grads = jnp.concatenate(grads, 0)
    rows = outs[0].shape[1]
    for start in range(0, activations_ref.shape[1], TILE):
        where = slice(start, start + TILE)
        value = jnp.dot(grads, activations_ref[:, where], preferred_element_type=F32)
        first = 0
        for out_ref in outs:
            for block in range(out_ref.shape[0]):
                out_ref[block, :, where] = value[first : first + rows].astype(out_ref.dtype)
                first += rows
        best = magnitude(value, best)
    return best


def multiply_even(place_ref, grads_ref, activations_ref, other_out, own_out, top_out):
    core, y = core_and_y(place_ref)
    grads = []
    for adder in (1 - core, core):
        for which in range(2):
            grads.append(grads_ref[block_of(adder, 0, which, y)[1] // 2])
    top_out[...] = multiply(grads, activations_ref, None, other_out, own_out)


def multiply_odd(of_other, place_ref, low_ref, high_ref, activations_ref, top_ref, out_ref, top_out):
    core, y = core_and_y(place_ref)
    grads = []
    for which in range(2):
        block = block_of(1 - core if of_other else core, 1, which, y)[1] // 2
        grads.append(jnp.where(block < 2, low_ref[block % 2], high_ref[block % 2]))
    top_out[...] = multiply(grads, activations_ref, top_ref[...], out_ref)


def add_cores(place_ref, own_even_ref, own_odd_ref, other_even_ref, other_odd_ref, out_ref):
    core, y = core_and_y(place_ref)
    for odd, own_ref, other_ref in ((0, own_even_ref, other_even_ref), (1, own_odd_ref, other_odd_ref)):
        for which in range(2):
            x = block_of(core, odd, which, y)[0]
            out_ref[x] = (own_ref[which] + other_ref[which].astype(F32)).astype(BF16)


def add_and_cut(place_ref, parts_ref, out_ref):
    y = core_and_y(place_ref)[1]
    rows = parts_ref.shape[1]

    def total(tile):
        where = slice(tile * LANES, (tile + 1) * LANES)
        value = parts_ref[0, :, where].astype(F32)
        for part in range(1, parts_ref.shape[0]):
            value += parts_ref[part, :, where].astype(F32)
        return value

    for pair in range(out_ref.shape[0] // 2):
        middle = total(3 * pair + 1)
        for odd in range(2):
            slot = slot_of(2 * pair + odd, y)
            out_ref[slot, :rows] = total(3 * pair + 2 * odd).astype(BF16)
            out_ref[slot, rows:] = fold(middle, odd).astype(BF16)


def adam_step(
    devices, place_ref, range_ref, summed_ref, top_ref, master_ref, moment_ref, second_ref,
    master_out, second_out, moment_out, sent_out,
):
    rows = master_ref.shape[0]
    is_even = core_and_y(place_ref)[0] == 0
    own, tail = summed_ref[:rows], summed_ref[rows:]
    middle = unfold(tail, tail)
    gradient = jnp.where(
        is_even,
        jnp.concatenate([own, middle[:, :HALF]], 1),
        jnp.concatenate([middle[:, HALF:], own], 1),
    ) / devices
    moment = (
        BETA_ONE * (moment_ref[...].astype(F32) * range_ref[0]) + (1.0 - BETA_ONE) * gradient
    )
    second_new = BETA_TWO * second_ref[...] + (1.0 - BETA_TWO) * gradient * gradient
    master = master_ref[...]
    master_new = master - LEARN_RATE * (
        moment / (jnp.sqrt(second_new) + ADAM_EPSILON) + DECAY_RATE * master
    )
    master_out[...] = master_new
    second_out[...] = second_new
    moment_out[...] = moment
    own = jnp.where(is_even, master_new[:, :LANES], master_new[:, HALF:]).astype(BF16)
    middle = jnp.concatenate([master_new[:, LANES:], master_new[:, :HALF]], 1)
    tail = jnp.where(is_even, fold(middle, False), fold(middle, True)).astype(BF16)
    row = lax.broadcasted_iota(jnp.int32, (8, LANES), 0)
    tops = (largest(top_ref[...]), largest(moment), largest(master_new))
    spread = split(jnp.where(row == 0, tops[0], jnp.where(row == 1, tops[1], tops[2])))
    for copy in range(sent_out.shape[0]):
        sent_out[copy, :rows] = own
        sent_out[copy, rows : rows + rows // 2] = tail
        sent_out[copy, rows + rows // 2 :] = spread


def join_blocks(held_ref, out_ref):
    packed = held_ref.shape[1] - TOP_ROWS
    best = None
    for z in range(held_ref.shape[0]):
        out_ref[z * packed : (z + 1) * packed] = held_ref[z, :packed]
        top = joined(held_ref[z, packed:])
        best = top if best is None else jnp.maximum(best, top)
    out_ref[held_ref.shape[0] * packed :] = split(best)


def join_tops(held_ref, out_ref):
    packed = held_ref.shape[1] - TOP_ROWS
    best = joined(held_ref[0, packed:])
    for x in range(1, held_ref.shape[0]):
        best = jnp.maximum(best, joined(held_ref[x, packed:]))
    for copy in range(out_ref.shape[0]):
        out_ref[copy] = best


def scale_weights(
    place_ref, tops_ref, own_ref, other_ref, moment_ref,
    weight_out, moment_out, moment_span_out, weight_span_out, grad_span_out, span_ref,
):
    rows = weight_out.shape[0]
    packed = rows + rows // 2
    step = pl.program_id(0)
    is_even = core_and_y(place_ref)[0] == 0

    @pl.when(step == 0)
    def _():
        best = tops_ref[0]
        for place in range(1, tops_ref.shape[0]):
            best = jnp.maximum(best, tops_ref[place])
        spans = best + EPSILON
        span_ref[...] = spans
        moment_out[...] = (moment_ref[...] / largest(spans[1:2])).astype(BF16)
        grad_span_out[0] = jnp.max(spans[0:1])
        moment_span_out[0] = jnp.max(spans[1:2])
        weight_span_out[0] = jnp.max(spans[2:3])

    scale = 1.0 / span_ref[2:3]
    for place in range((own_ref.shape[1] - TOP_ROWS) // packed):
        where = slice(place * packed, (place + 1) * packed)
        own = own_ref[step, where].astype(F32) * scale
        other = other_ref[step, where].astype(F32) * scale
        even, odd = jnp.where(is_even, own, other), jnp.where(is_even, other, own)
        start = 3 * LANES * place
        weight_out[:, start : start + LANES] = even[:rows].astype(BF16)
        weight_out[:, start + LANES : start + 2 * LANES] = unfold(even[rows:], odd[rows:]).astype(BF16)
        weight_out[:, start + 2 * LANES : start + 3 * LANES] = odd[:rows].astype(BF16)


def on_device(activations, output_grads, master, moment_q, moment_range, second_moment):
    xs, zs, cores, ys = (lax.axis_size(name) for name in DEVICE)
    rows, width = master.shape
    packed = rows + rows // 2
    sent_rows = packed + TOP_ROWS
    place = lax.axis_index(("core", "y")).reshape(1)
    output_grads, place = lax.optimization_barrier((output_grads, place))
    swap = [(0, 1), (1, 0)]

    tokens, columns = output_grads.shape
    every_second = [list(range(first, ys, 2)) for first in range(2)]
    even = lax.all_gather(output_grads.T, "y", axis_index_groups=every_second)
    low = lax.ppermute(even[: ys // 4], "y", [(y, (y - 1) % ys) for y in range(ys)])
    high = lax.ppermute(even[ys // 4 :], "y", [(y, (y + 1) % ys) for y in range(ys)])

    def product(dtype):
        return jax.ShapeDtypeStruct((2, columns, activations.shape[1]), dtype)

    top_shape = jax.ShapeDtypeStruct((8, LANES), F32)
    to_other_even, own_even, top = pl.pallas_call(
        multiply_even,
        out_shape=(product(BF16), product(F32), top_shape),
        in_specs=[SMEM, VMEM, VMEM],
        out_specs=(VMEM,) * 3,
        compiler_params=grant(14),
    )(place, even, activations)
    to_other_odd, top = pl.pallas_call(
        functools.partial(multiply_odd, True),
        out_shape=(product(BF16), top_shape),
        in_specs=[SMEM] + [VMEM] * 4,
        out_specs=(VMEM, VMEM),
        compiler_params=grant(14),
    )(place, low, high, activations, top)
    own_odd, top = pl.pallas_call(
        functools.partial(multiply_odd, False),
        out_shape=(product(F32), top_shape),
        in_specs=[SMEM] + [VMEM] * 4,
        out_specs=(VMEM, VMEM),
        compiler_params=grant(14),
    )(place, low, high, activations, top)

    other_even = lax.ppermute(to_other_even, "core", swap)
    other_odd = lax.ppermute(to_other_odd, "core", swap)
    value = pl.pallas_call(
        add_cores,
        out_shape=jax.ShapeDtypeStruct((xs, rows, activations.shape[1]), BF16),
        in_specs=[SMEM] + [VMEM] * 4,
        out_specs=VMEM,
        compiler_params=grant(10),
    )(place, own_even, own_odd, other_even, other_odd)
    value = lax.all_to_all(value, "x", 0, 0, tiled=True)
    value = pl.pallas_call(
        add_and_cut,
        out_shape=jax.ShapeDtypeStruct((zs, packed, LANES), BF16),
        in_specs=[SMEM, VMEM],
        out_specs=VMEM,
        compiler_params=grant(4),
    )(place, value)
    value = lax.all_to_all(value, "z", 0, 0, tiled=True)
    value = jnp.sum(value.astype(F32), axis=0)
    route = []
    for half in range(cores):
        for odd in range(2):
            for which in range(2):
                for y in range(ys):
                    x, column = block_of(half, odd, which, y)
                    for feature in range(zs):
                        source = ((x * zs + slot_of(feature, y)) * cores + half) * ys + y
                        route.append((source, (y * zs + feature) * ys + column))
    value = lax.ppermute(value, DEVICE, route)

    block = jax.ShapeDtypeStruct((rows, width), F32)
    master_new, second_new, moment, held = pl.pallas_call(
        functools.partial(adam_step, xs * zs * cores),
        out_shape=(block, block, block, jax.ShapeDtypeStruct((zs, sent_rows, LANES), BF16)),
        in_specs=[SMEM, SMEM] + [VMEM] * 5,
        out_specs=(VMEM,) * 4,
        compiler_params=grant(4),
    )(place, moment_range, value, top, master, moment_q, second_moment)

    held = lax.all_to_all(held, "z", 0, 0, tiled=True)
    held = pl.pallas_call(
        join_blocks,
        out_shape=jax.ShapeDtypeStruct((zs * packed + TOP_ROWS, LANES), BF16),
        in_specs=[VMEM],
        out_specs=VMEM,
        compiler_params=grant(4),
    )(held)
    held = lax.all_gather(held, "x")
    other = lax.ppermute(held, "core", swap)
    tops = pl.pallas_call(
        join_tops,
        out_shape=jax.ShapeDtypeStruct((cores * ys, 8, LANES), F32),
        in_specs=[VMEM],
        out_specs=VMEM,
        compiler_params=grant(4),
    )(held)
    tops = lax.all_to_all(tops, ("core", "y"), 0, 0, tiled=True)

    one = jax.ShapeDtypeStruct((1,), F32)
    weight_q, moment_q_new, moment_span, weight_span, grad_span = pl.pallas_call(
        scale_weights,
        grid=(xs,),
        out_shape=(
            jax.ShapeDtypeStruct((rows, width * xs * zs * cores), BF16),
            jax.ShapeDtypeStruct((rows, width), BF16),
            one,
            one,
            one,
        ),
        in_specs=[SMEM, VMEM, VMEM, VMEM, VMEM],
        out_specs=(
            pl.BlockSpec((rows, width * zs * cores), lambda i: (0, i)),
            VMEM,
            SMEM,
            SMEM,
            SMEM,
        ),
        scratch_shapes=[pltpu.VMEM((8, LANES), F32)],
        compiler_params=grant(8),
    )(place, tops, held, other, moment)
    return master_new, moment_q_new, moment_span, second_new, weight_q, weight_span, grad_span


def solution(mesh):
    inner = Mesh(mesh.devices.reshape(4, 8, 2, 8), DEVICE)
    dp, mp = ("x", "z", "core"), "y"
    placed = (P(dp, mp), P(dp, mp), P(mp, dp), P(mp, dp), P(), P(mp, dp))
    return jax.shard_map(
        on_device,
        mesh=inner,
        in_specs=placed,
        out_specs=(P(mp, dp), P(mp, dp), P(), P(mp, dp), P(mp, None), P(), P()),
        check_vma=False,
    )
```

```python
import functools

import jax
import jax.numpy as jnp
from jax import lax
from jax.experimental import pallas as pl
from jax.experimental.pallas import tpu as pltpu
from jax.sharding import Mesh, PartitionSpec as P

EPSILON = 1e-06
BETA_ONE = 0.9
BETA_TWO = 0.999
LEARN_RATE = 0.001
DECAY_RATE = 0.1
ADAM_EPSILON = 1e-08

F32 = jnp.float32
BF16 = jnp.bfloat16
LANES = 128
HALF = LANES // 2
TOP_ROWS = 16
TILE = 512
DEVICE = ("x", "z", "core", "y")
SMEM = pl.BlockSpec(memory_space=pltpu.SMEM)
VMEM = pl.BlockSpec(memory_space=pltpu.VMEM)
MIB = 1024 * 1024


def grant(size):
    return pltpu.CompilerParams(vmem_limit_bytes=size * MIB)


def fold(middle, odd):
    rows = middle.shape[0] // 2
    upper, lower = middle[:rows], pltpu.roll(middle[rows:], HALF, 1)
    left = lax.broadcasted_iota(jnp.int32, upper.shape, 1) < HALF
    return jnp.where(left, lower, upper) if odd else jnp.where(left, upper, lower)


def unfold(even_tail, odd_tail):
    left = lax.broadcasted_iota(jnp.int32, even_tail.shape, 1) < HALF
    upper = jnp.where(left, even_tail, odd_tail)
    lower = pltpu.roll(jnp.where(left, odd_tail, even_tail), HALF, 1)
    return jnp.concatenate([upper, lower], 0)


def largest(value):
    return jnp.max(jnp.max(jnp.abs(value), axis=1, keepdims=True), axis=0, keepdims=True)


def magnitude(value, best):
    top = jnp.max(jnp.abs(value).reshape(-1, 8, value.shape[1]), axis=0)
    for start in range(0, value.shape[1], LANES):
        part = top[:, start : start + LANES]
        best = part if best is None else jnp.maximum(best, part)
    return best


def split(top):
    high = top.astype(BF16).astype(F32)
    middle = (top - high).astype(BF16).astype(F32)
    low = top - high - middle
    row = lax.broadcasted_iota(jnp.int32, top.shape, 0)
    high = jnp.where(row < 4, high, pltpu.roll(low, 4, 0))
    return jnp.concatenate([high, middle], 0).astype(BF16)


def joined(spread):
    spread = spread.astype(F32)
    return spread[:8] + spread[8:] + pltpu.roll(spread[:8], 4, 0)


ABOVE = (((4, 0), (-1, 3)), ((2, -2), (-3, 1)))


def block_of(core, odd, which, y):
    place = (core + odd) % 2 + 2 * which
    if isinstance(core, int):
        above = ABOVE[core][odd][which]
    else:
        above = jnp.where(core == 0, ABOVE[0][odd][which], ABOVE[1][odd][which])
    return (place + y // 2) % 4, (y + above + 8) % 8


def slot_of(feature, y):
    return (feature + 6 + 4 * (y % 2)) % 8


def core_and_y(place_ref):
    return place_ref[0] // 8, place_ref[0] % 8


def multiply(grads, activations_ref, best, *outs):
    grads = jnp.concatenate(grads, 0)
    rows = outs[0].shape[1]
    for start in range(0, activations_ref.shape[1], TILE):
        where = slice(start, start + TILE)
        value = jnp.dot(grads, activations_ref[:, where], preferred_element_type=F32)
        first = 0
        for out_ref in outs:
            for block in range(out_ref.shape[0]):
                out_ref[block, :, where] = value[first : first + rows].astype(out_ref.dtype)
                first += rows
        best = magnitude(value, best)
    return best


def multiply_even(place_ref, grads_ref, activations_ref, other_out, own_out, top_out):
    core, y = core_and_y(place_ref)
    grads = []
    for adder in (1 - core, core):
        for which in range(2):
            grads.append(grads_ref[block_of(adder, 0, which, y)[1] // 2])
    top_out[...] = multiply(grads, activations_ref, None, other_out, own_out)


def multiply_odd(of_other, place_ref, low_ref, high_ref, activations_ref, top_ref, out_ref, top_out):
    core, y = core_and_y(place_ref)
    grads = []
    for which in range(2):
        block = block_of(1 - core if of_other else core, 1, which, y)[1] // 2
        grads.append(jnp.where(block < 2, low_ref[block % 2], high_ref[block % 2]))
    top_out[...] = multiply(grads, activations_ref, top_ref[...], out_ref)


def add_cores(place_ref, own_even_ref, own_odd_ref, other_even_ref, other_odd_ref, out_ref):
    core, y = core_and_y(place_ref)
    for odd, own_ref, other_ref in ((0, own_even_ref, other_even_ref), (1, own_odd_ref, other_odd_ref)):
        for which in range(2):
            x = block_of(core, odd, which, y)[0]
            out_ref[x] = (own_ref[which] + other_ref[which].astype(F32)).astype(BF16)


def add_and_cut(place_ref, parts_ref, out_ref):
    y = core_and_y(place_ref)[1]
    rows = parts_ref.shape[1]

    def total(tile):
        where = slice(tile * LANES, (tile + 1) * LANES)
        value = parts_ref[0, :, where].astype(F32)
        for part in range(1, parts_ref.shape[0]):
            value += parts_ref[part, :, where].astype(F32)
        return value

    for pair in range(out_ref.shape[0] // 2):
        middle = total(3 * pair + 1)
        for odd in range(2):
            slot = slot_of(2 * pair + odd, y)
            out_ref[slot, :rows] = total(3 * pair + 2 * odd).astype(BF16)
            out_ref[slot, rows:] = fold(middle, odd).astype(BF16)


def adam_step(
    devices, place_ref, range_ref, summed_ref, top_ref, master_ref, moment_ref, second_ref,
    master_out, second_out, moment_out, sent_out,
):
    rows = master_ref.shape[0]
    is_even = core_and_y(place_ref)[0] == 0
    own, tail = summed_ref[:rows], summed_ref[rows:]
    middle = unfold(tail, tail)
    gradient = jnp.where(
        is_even,
        jnp.concatenate([own, middle[:, :HALF]], 1),
        jnp.concatenate([middle[:, HALF:], own], 1),
    ) / devices
    moment = (
        BETA_ONE * (moment_ref[...].astype(F32) * range_ref[0]) + (1.0 - BETA_ONE) * gradient
    )
    second_new = BETA_TWO * second_ref[...] + (1.0 - BETA_TWO) * gradient * gradient
    master = master_ref[...]
    master_new = master - LEARN_RATE * (
        moment / (jnp.sqrt(second_new) + ADAM_EPSILON) + DECAY_RATE * master
    )
    master_out[...] = master_new
    second_out[...] = second_new
    moment_out[...] = moment
    own = jnp.where(is_even, master_new[:, :LANES], master_new[:, HALF:]).astype(BF16)
    middle = jnp.concatenate([master_new[:, LANES:], master_new[:, :HALF]], 1)
    tail = jnp.where(is_even, fold(middle, False), fold(middle, True)).astype(BF16)
    row = lax.broadcasted_iota(jnp.int32, (8, LANES), 0)
    tops = (largest(top_ref[...]), largest(moment), largest(master_new))
    spread = split(jnp.where(row == 0, tops[0], jnp.where(row == 1, tops[1], tops[2])))
    for copy in range(sent_out.shape[0]):
        sent_out[copy, :rows] = own
        sent_out[copy, rows : rows + rows // 2] = tail
        sent_out[copy, rows + rows // 2 :] = spread


def join_blocks(held_ref, out_ref):
    packed = held_ref.shape[1] - TOP_ROWS
    best = None
    for z in range(held_ref.shape[0]):
        out_ref[z * packed : (z + 1) * packed] = held_ref[z, :packed]
        top = joined(held_ref[z, packed:])
        best = top if best is None else jnp.maximum(best, top)
    out_ref[held_ref.shape[0] * packed :] = split(best)


def join_tops(held_ref, out_ref):
    packed = held_ref.shape[1] - TOP_ROWS
    best = joined(held_ref[0, packed:])
    for x in range(1, held_ref.shape[0]):
        best = jnp.maximum(best, joined(held_ref[x, packed:]))
    for copy in range(out_ref.shape[0]):
        out_ref[copy] = best


def lay_out(place_ref, own_ref, other_ref, out_ref):
    rows = out_ref.shape[0]
    packed = rows + rows // 2
    is_even = core_and_y(place_ref)[0] == 0

    def fill(even_ref, odd_ref):
        blocks = (even_ref.shape[1] - TOP_ROWS) // packed
        for place in range(even_ref.shape[0] * blocks):
            x, start = place // blocks, place % blocks * packed
            tails = slice(start + rows, start + packed)
            middle = unfold(even_ref[x, tails].astype(F32), odd_ref[x, tails].astype(F32))
            column = 3 * LANES * place
            out_ref[:, column : column + LANES] = even_ref[x, start : start + rows]
            out_ref[:, column + LANES : column + 2 * LANES] = middle.astype(BF16)
            out_ref[:, column + 2 * LANES : column + 3 * LANES] = odd_ref[x, start : start + rows]

    pl.when(is_even)(lambda: fill(own_ref, other_ref))
    pl.when(jnp.logical_not(is_even))(lambda: fill(other_ref, own_ref))


def scale_weights(
    tops_ref, laid_ref, moment_ref,
    weight_out, moment_out, moment_span_out, weight_span_out, grad_span_out, span_ref,
):
    step = pl.program_id(0)

    @pl.when(step == 0)
    def _():
        best = tops_ref[0]
        for place in range(1, tops_ref.shape[0]):
            best = jnp.maximum(best, tops_ref[place])
        spans = best + EPSILON
        span_ref[...] = 1.0 / spans
        moment_out[...] = (moment_ref[...] / largest(spans[1:2])).astype(BF16)
        grad_span_out[0] = jnp.max(spans[0:1])
        moment_span_out[0] = jnp.max(spans[1:2])
        weight_span_out[0] = jnp.max(spans[2:3])

    scale = span_ref[2:3]
    width = weight_out.shape[1]
    for start in range(0, width, LANES):
        where = pl.ds(pl.multiple_of(step * width + start, LANES), LANES)
        weight_out[:, start : start + LANES] = (laid_ref[:, where].astype(F32) * scale).astype(BF16)


def on_device(activations, output_grads, master, moment_q, moment_range, second_moment):
    xs, zs, cores, ys = (lax.axis_size(name) for name in DEVICE)
    rows, width = master.shape
    packed = rows + rows // 2
    sent_rows = packed + TOP_ROWS
    place = lax.axis_index(("core", "y")).reshape(1)
    output_grads, place = lax.optimization_barrier((output_grads, place))
    swap = [(0, 1), (1, 0)]

    tokens, columns = output_grads.shape
    every_second = [list(range(first, ys, 2)) for first in range(2)]
    even = lax.all_gather(output_grads.T, "y", axis_index_groups=every_second)
    low = lax.ppermute(even[: ys // 4], "y", [(y, (y - 1) % ys) for y in range(ys)])
    high = lax.ppermute(even[ys // 4 :], "y", [(y, (y + 1) % ys) for y in range(ys)])

    def product(dtype):
        return jax.ShapeDtypeStruct((2, columns, activations.shape[1]), dtype)

    top_shape = jax.ShapeDtypeStruct((8, LANES), F32)
    to_other_even, own_even, top = pl.pallas_call(
        multiply_even,
        out_shape=(product(BF16), product(F32), top_shape),
        in_specs=[SMEM, VMEM, VMEM],
        out_specs=(VMEM,) * 3,
        compiler_params=grant(14),
    )(place, even, activations)
    to_other_odd, top = pl.pallas_call(
        functools.partial(multiply_odd, True),
        out_shape=(product(BF16), top_shape),
        in_specs=[SMEM] + [VMEM] * 4,
        out_specs=(VMEM, VMEM),
        compiler_params=grant(14),
    )(place, low, high, activations, top)
    own_odd, top = pl.pallas_call(
        functools.partial(multiply_odd, False),
        out_shape=(product(F32), top_shape),
        in_specs=[SMEM] + [VMEM] * 4,
        out_specs=(VMEM, VMEM),
        compiler_params=grant(14),
    )(place, low, high, activations, top)

    other_even = lax.ppermute(to_other_even, "core", swap)
    other_odd = lax.ppermute(to_other_odd, "core", swap)
    value = pl.pallas_call(
        add_cores,
        out_shape=jax.ShapeDtypeStruct((xs, rows, activations.shape[1]), BF16),
        in_specs=[SMEM] + [VMEM] * 4,
        out_specs=VMEM,
        compiler_params=grant(10),
    )(place, own_even, own_odd, other_even, other_odd)
    value = lax.all_to_all(value, "x", 0, 0, tiled=True)
    value = pl.pallas_call(
        add_and_cut,
        out_shape=jax.ShapeDtypeStruct((zs, packed, LANES), BF16),
        in_specs=[SMEM, VMEM],
        out_specs=VMEM,
        compiler_params=grant(4),
    )(place, value)
    value = lax.all_to_all(value, "z", 0, 0, tiled=True)
    value = jnp.sum(value.astype(F32), axis=0)
    route = []
    for half in range(cores):
        for odd in range(2):
            for which in range(2):
                for y in range(ys):
                    x, column = block_of(half, odd, which, y)
                    for feature in range(zs):
                        source = ((x * zs + slot_of(feature, y)) * cores + half) * ys + y
                        route.append((source, (y * zs + feature) * ys + column))
    value = lax.ppermute(value, DEVICE, route)

    block = jax.ShapeDtypeStruct((rows, width), F32)
    master_new, second_new, moment, held = pl.pallas_call(
        functools.partial(adam_step, xs * zs * cores),
        out_shape=(block, block, block, jax.ShapeDtypeStruct((zs, sent_rows, LANES), BF16)),
        in_specs=[SMEM, SMEM] + [VMEM] * 5,
        out_specs=(VMEM,) * 4,
        compiler_params=grant(4),
    )(place, moment_range, value, top, master, moment_q, second_moment)

    held = lax.all_to_all(held, "z", 0, 0, tiled=True)
    held = pl.pallas_call(
        join_blocks,
        out_shape=jax.ShapeDtypeStruct((zs * packed + TOP_ROWS, LANES), BF16),
        in_specs=[VMEM],
        out_specs=VMEM,
        compiler_params=grant(4),
    )(held)
    held = lax.all_gather(held, "x")
    other = lax.ppermute(held, "core", swap)
    tops = pl.pallas_call(
        join_tops,
        out_shape=jax.ShapeDtypeStruct((cores * ys, 8, LANES), F32),
        in_specs=[VMEM],
        out_specs=VMEM,
        compiler_params=grant(4),
    )(held)
    tops = lax.all_to_all(tops, ("core", "y"), 0, 0, tiled=True)

    whole = jax.ShapeDtypeStruct((rows, width * xs * zs * cores), BF16)
    laid = pl.pallas_call(
        lay_out,
        out_shape=whole,
        in_specs=[SMEM, VMEM, VMEM],
        out_specs=VMEM,
        compiler_params=grant(8),
    )(place, held, other)

    one = jax.ShapeDtypeStruct((1,), F32)
    weight_q, moment_q_new, moment_span, weight_span, grad_span = pl.pallas_call(
        scale_weights,
        grid=(xs,),
        out_shape=(whole, jax.ShapeDtypeStruct((rows, width), BF16), one, one, one),
        in_specs=[VMEM, VMEM, VMEM],
        out_specs=(
            pl.BlockSpec((rows, width * zs * cores), lambda i: (0, i)),
            VMEM,
            SMEM,
            SMEM,
            SMEM,
        ),
        scratch_shapes=[pltpu.VMEM((8, LANES), F32)],
        compiler_params=grant(8),
    )(tops, laid, moment)
    return master_new, moment_q_new, moment_span, second_new, weight_q, weight_span, grad_span


def solution(mesh):
    inner = Mesh(mesh.devices.reshape(4, 8, 2, 8), DEVICE)
    dp, mp = ("x", "z", "core"), "y"
    placed = (P(dp, mp), P(dp, mp), P(mp, dp), P(mp, dp), P(), P(mp, dp))
    return jax.shard_map(
        on_device,
        mesh=inner,
        in_specs=placed,
        out_specs=(P(mp, dp), P(mp, dp), P(), P(mp, dp), P(mp, None), P(), P()),
        check_vma=False,
    )
```

```python
import functools

import jax
import jax.numpy as jnp
from jax import lax
from jax.experimental import pallas as pl
from jax.experimental.pallas import tpu as pltpu
from jax.sharding import Mesh, PartitionSpec as P

EPSILON = 1e-06
BETA_ONE = 0.9
BETA_TWO = 0.999
LEARN_RATE = 0.001
DECAY_RATE = 0.1
ADAM_EPSILON = 1e-08

F32 = jnp.float32
BF16 = jnp.bfloat16
LANES = 128
HALF = LANES // 2
TOP_ROWS = 16
TILE = 512
DEVICE = ("x", "z", "core", "y")
SMEM = pl.BlockSpec(memory_space=pltpu.SMEM)
VMEM = pl.BlockSpec(memory_space=pltpu.VMEM)
MIB = 1024 * 1024


def grant(size):
    return pltpu.CompilerParams(vmem_limit_bytes=size * MIB)


def fold(middle, odd):
    rows = middle.shape[0] // 2
    upper, lower = middle[:rows], pltpu.roll(middle[rows:], HALF, 1)
    left = lax.broadcasted_iota(jnp.int32, upper.shape, 1) < HALF
    return jnp.where(left, lower, upper) if odd else jnp.where(left, upper, lower)


def unfold(even_tail, odd_tail):
    left = lax.broadcasted_iota(jnp.int32, even_tail.shape, 1) < HALF
    upper = jnp.where(left, even_tail, odd_tail)
    lower = pltpu.roll(jnp.where(left, odd_tail, even_tail), HALF, 1)
    return jnp.concatenate([upper, lower], 0)


def largest(value):
    return jnp.max(jnp.max(jnp.abs(value), axis=1, keepdims=True), axis=0, keepdims=True)


def magnitude(value, best):
    top = jnp.max(jnp.abs(value).reshape(-1, 8, value.shape[1]), axis=0)
    for start in range(0, value.shape[1], LANES):
        part = top[:, start : start + LANES]
        best = part if best is None else jnp.maximum(best, part)
    return best


def split(top):
    high = top.astype(BF16).astype(F32)
    middle = (top - high).astype(BF16).astype(F32)
    low = top - high - middle
    row = lax.broadcasted_iota(jnp.int32, top.shape, 0)
    high = jnp.where(row < 4, high, pltpu.roll(low, 4, 0))
    return jnp.concatenate([high, middle], 0).astype(BF16)


def joined(spread):
    spread = spread.astype(F32)
    return spread[:8] + spread[8:] + pltpu.roll(spread[:8], 4, 0)


ABOVE = (((4, 0), (-1, 3)), ((2, -2), (-3, 1)))


def block_of(core, odd, which, y):
    place = (core + odd) % 2 + 2 * which
    if isinstance(core, int):
        above = ABOVE[core][odd][which]
    else:
        above = jnp.where(core == 0, ABOVE[0][odd][which], ABOVE[1][odd][which])
    return (place + y // 2) % 4, (y + above + 8) % 8


def slot_of(feature, y):
    return (feature + 6 + 4 * (y % 2)) % 8


def core_and_y(place_ref):
    return place_ref[0] // 8, place_ref[0] % 8


def multiply(grads, activations_ref, best, *outs):
    grads = jnp.concatenate(grads, 0)
    rows = outs[0].shape[1]
    for start in range(0, activations_ref.shape[1], TILE):
        where = slice(start, start + TILE)
        value = jnp.dot(grads, activations_ref[:, where], preferred_element_type=F32)
        first = 0
        for out_ref in outs:
            for block in range(out_ref.shape[0]):
                out_ref[block, :, where] = value[first : first + rows].astype(out_ref.dtype)
                first += rows
        best = magnitude(value, best)
    return best


def multiply_even(place_ref, grads_ref, activations_ref, other_out, own_out, top_out):
    core, y = core_and_y(place_ref)
    grads = []
    for adder in (1 - core, core):
        for which in range(2):
            grads.append(grads_ref[block_of(adder, 0, which, y)[1] // 2])
    top_out[...] = multiply(grads, activations_ref, None, other_out, own_out)


def multiply_odd(of_other, place_ref, low_ref, high_ref, activations_ref, top_ref, out_ref, top_out):
    core, y = core_and_y(place_ref)
    grads = []
    for which in range(2):
        block = block_of(1 - core if of_other else core, 1, which, y)[1] // 2
        grads.append(jnp.where(block < 2, low_ref[block % 2], high_ref[block % 2]))
    top_out[...] = multiply(grads, activations_ref, top_ref[...], out_ref)


def add_cores(place_ref, own_even_ref, own_odd_ref, other_even_ref, other_odd_ref, out_ref):
    core, y = core_and_y(place_ref)
    for odd, own_ref, other_ref in ((0, own_even_ref, other_even_ref), (1, own_odd_ref, other_odd_ref)):
        for which in range(2):
            x = block_of(core, odd, which, y)[0]
            out_ref[x] = (own_ref[which] + other_ref[which].astype(F32)).astype(BF16)


def add_and_cut(place_ref, parts_ref, out_ref):
    y = core_and_y(place_ref)[1]
    rows = parts_ref.shape[1]

    def total(tile):
        where = slice(tile * LANES, (tile + 1) * LANES)
        value = parts_ref[0, :, where].astype(F32)
        for part in range(1, parts_ref.shape[0]):
            value += parts_ref[part, :, where].astype(F32)
        return value

    for pair in range(out_ref.shape[0] // 2):
        middle = total(3 * pair + 1)
        for odd in range(2):
            slot = slot_of(2 * pair + odd, y)
            out_ref[slot, :rows] = total(3 * pair + 2 * odd).astype(BF16)
            out_ref[slot, rows:] = fold(middle, odd).astype(BF16)


def adam_step(
    devices, place_ref, range_ref, summed_ref, top_ref, master_ref, moment_ref, second_ref,
    master_out, second_out, moment_out, sent_out,
):
    rows = master_ref.shape[0]
    is_even = core_and_y(place_ref)[0] == 0
    own, tail = summed_ref[:rows], summed_ref[rows:]
    middle = unfold(tail, tail)
    gradient = jnp.where(
        is_even,
        jnp.concatenate([own, middle[:, :HALF]], 1),
        jnp.concatenate([middle[:, HALF:], own], 1),
    ) / devices
    moment = (
        BETA_ONE * (moment_ref[...].astype(F32) * range_ref[0]) + (1.0 - BETA_ONE) * gradient
    )
    second_new = BETA_TWO * second_ref[...] + (1.0 - BETA_TWO) * gradient * gradient
    master = master_ref[...]
    master_new = master - LEARN_RATE * (
        moment / (jnp.sqrt(second_new) + ADAM_EPSILON) + DECAY_RATE * master
    )
    master_out[...] = master_new
    second_out[...] = second_new
    moment_out[...] = moment
    own = jnp.where(is_even, master_new[:, :LANES], master_new[:, HALF:]).astype(BF16)
    middle = jnp.concatenate([master_new[:, LANES:], master_new[:, :HALF]], 1)
    tail = jnp.where(is_even, fold(middle, False), fold(middle, True)).astype(BF16)
    row = lax.broadcasted_iota(jnp.int32, (8, LANES), 0)
    tops = (largest(top_ref[...]), largest(moment), largest(master_new))
    spread = split(jnp.where(row == 0, tops[0], jnp.where(row == 1, tops[1], tops[2])))
    for copy in range(sent_out.shape[0]):
        sent_out[copy, :rows] = own
        sent_out[copy, rows : rows + rows // 2] = tail
        sent_out[copy, rows + rows // 2 :] = spread


def join_blocks(held_ref, out_ref):
    packed = held_ref.shape[1] - TOP_ROWS
    best = None
    for z in range(held_ref.shape[0]):
        out_ref[z * packed : (z + 1) * packed] = held_ref[z, :packed]
        top = joined(held_ref[z, packed:])
        best = top if best is None else jnp.maximum(best, top)
    out_ref[held_ref.shape[0] * packed :] = split(best)


def join_tops(held_ref, out_ref):
    packed = held_ref.shape[1] - TOP_ROWS
    best = joined(held_ref[0, packed:])
    for x in range(1, held_ref.shape[0]):
        best = jnp.maximum(best, joined(held_ref[x, packed:]))
    for copy in range(out_ref.shape[0]):
        out_ref[copy] = best


def scale_weights(
    place_ref, tops_ref, own_ref, other_ref, moment_ref,
    weight_out, moment_out, moment_span_out, weight_span_out, grad_span_out, scaled_ref, written,
):
    rows = moment_ref.shape[0]
    packed = rows + rows // 2
    is_even = core_and_y(place_ref)[0] == 0
    best = tops_ref[0]
    for place in range(1, tops_ref.shape[0]):
        best = jnp.maximum(best, tops_ref[place])
    spans = best + EPSILON
    scale = (1.0 / spans)[2:3]
    copies = []
    for x in range(own_ref.shape[0]):
        blocks = (own_ref.shape[1] - TOP_ROWS) // packed
        for place in range(blocks):
            where = slice(place * packed, (place + 1) * packed)
            own = own_ref[x, where].astype(F32) * scale
            other = other_ref[x, where].astype(F32) * scale
            even, odd = jnp.where(is_even, own, other), jnp.where(is_even, other, own)
            tiles = (even[:rows], unfold(even[rows:], odd[rows:]), odd[:rows])
            for tile, value in enumerate(tiles):
                start = LANES * (3 * (x * blocks + place) + tile)
                scaled_ref[:, start : start + LANES] = value.astype(BF16)
        where = slice(3 * LANES * blocks * x, 3 * LANES * blocks * (x + 1))
        copies.append(pltpu.make_async_copy(scaled_ref.at[:, where], weight_out.at[:, where], written.at[x]))
        copies[-1].start()
    moment_out[...] = (moment_ref[...] / largest(spans[1:2])).astype(BF16)
    grad_span_out[0] = jnp.max(spans[0:1])
    moment_span_out[0] = jnp.max(spans[1:2])
    weight_span_out[0] = jnp.max(spans[2:3])
    for copy in copies:
        copy.wait()


def on_device(activations, output_grads, master, moment_q, moment_range, second_moment):
    xs, zs, cores, ys = (lax.axis_size(name) for name in DEVICE)
    rows, width = master.shape
    packed = rows + rows // 2
    sent_rows = packed + TOP_ROWS
    place = lax.axis_index(("core", "y")).reshape(1)
    output_grads, place = lax.optimization_barrier((output_grads, place))
    swap = [(0, 1), (1, 0)]

    tokens, columns = output_grads.shape
    every_second = [list(range(first, ys, 2)) for first in range(2)]
    even = lax.all_gather(output_grads.T, "y", axis_index_groups=every_second)
    low = lax.ppermute(even[: ys // 4], "y", [(y, (y - 1) % ys) for y in range(ys)])
    high = lax.ppermute(even[ys // 4 :], "y", [(y, (y + 1) % ys) for y in range(ys)])

    def product(dtype):
        return jax.ShapeDtypeStruct((2, columns, activations.shape[1]), dtype)

    top_shape = jax.ShapeDtypeStruct((8, LANES), F32)
    to_other_even, own_even, top = pl.pallas_call(
        multiply_even,
        out_shape=(product(BF16), product(F32), top_shape),
        in_specs=[SMEM, VMEM, VMEM],
        out_specs=(VMEM,) * 3,
        compiler_params=grant(14),
    )(place, even, activations)
    to_other_odd, top = pl.pallas_call(
        functools.partial(multiply_odd, True),
        out_shape=(product(BF16), top_shape),
        in_specs=[SMEM] + [VMEM] * 4,
        out_specs=(VMEM, VMEM),
        compiler_params=grant(14),
    )(place, low, high, activations, top)
    own_odd, top = pl.pallas_call(
        functools.partial(multiply_odd, False),
        out_shape=(product(F32), top_shape),
        in_specs=[SMEM] + [VMEM] * 4,
        out_specs=(VMEM, VMEM),
        compiler_params=grant(14),
    )(place, low, high, activations, top)

    other_even = lax.ppermute(to_other_even, "core", swap)
    other_odd = lax.ppermute(to_other_odd, "core", swap)
    value = pl.pallas_call(
        add_cores,
        out_shape=jax.ShapeDtypeStruct((xs, rows, activations.shape[1]), BF16),
        in_specs=[SMEM] + [VMEM] * 4,
        out_specs=VMEM,
        compiler_params=grant(10),
    )(place, own_even, own_odd, other_even, other_odd)
    value = lax.all_to_all(value, "x", 0, 0, tiled=True)
    value = pl.pallas_call(
        add_and_cut,
        out_shape=jax.ShapeDtypeStruct((zs, packed, LANES), BF16),
        in_specs=[SMEM, VMEM],
        out_specs=VMEM,
        compiler_params=grant(4),
    )(place, value)
    value = lax.all_to_all(value, "z", 0, 0, tiled=True)
    value = jnp.sum(value.astype(F32), axis=0)
    route = []
    for half in range(cores):
        for odd in range(2):
            for which in range(2):
                for y in range(ys):
                    x, column = block_of(half, odd, which, y)
                    for feature in range(zs):
                        source = ((x * zs + slot_of(feature, y)) * cores + half) * ys + y
                        route.append((source, (y * zs + feature) * ys + column))
    value = lax.ppermute(value, DEVICE, route)

    block = jax.ShapeDtypeStruct((rows, width), F32)
    master_new, second_new, moment, held = pl.pallas_call(
        functools.partial(adam_step, xs * zs * cores),
        out_shape=(block, block, block, jax.ShapeDtypeStruct((zs, sent_rows, LANES), BF16)),
        in_specs=[SMEM, SMEM] + [VMEM] * 5,
        out_specs=(VMEM,) * 4,
        compiler_params=grant(4),
    )(place, moment_range, value, top, master, moment_q, second_moment)

    held = lax.all_to_all(held, "z", 0, 0, tiled=True)
    held = pl.pallas_call(
        join_blocks,
        out_shape=jax.ShapeDtypeStruct((zs * packed + TOP_ROWS, LANES), BF16),
        in_specs=[VMEM],
        out_specs=VMEM,
        compiler_params=grant(4),
    )(held)
    held = lax.all_gather(held, "x")
    tops = pl.pallas_call(
        join_tops,
        out_shape=jax.ShapeDtypeStruct((cores * ys, 8, LANES), F32),
        in_specs=[VMEM],
        out_specs=VMEM,
        compiler_params=grant(4),
    )(held)
    tops = lax.all_to_all(tops, ("core", "y"), 0, 0, tiled=True)
    other = lax.ppermute(held, "core", swap)

    one = jax.ShapeDtypeStruct((1,), F32)
    whole = jax.ShapeDtypeStruct((rows, width * xs * zs * cores), BF16)
    weight_q, moment_q_new, moment_span, weight_span, grad_span = pl.pallas_call(
        scale_weights,
        out_shape=(whole, jax.ShapeDtypeStruct((rows, width), BF16), one, one, one),
        in_specs=[SMEM] + [VMEM] * 4,
        out_specs=(pl.BlockSpec(memory_space=pl.ANY), VMEM, SMEM, SMEM, SMEM),
        scratch_shapes=[pltpu.VMEM(whole.shape, BF16), pltpu.SemaphoreType.DMA((xs,))],
        compiler_params=grant(8),
    )(place, tops, held, other, moment)
    return master_new, moment_q_new, moment_span, second_new, weight_q, weight_span, grad_span


def solution(mesh):
    inner = Mesh(mesh.devices.reshape(4, 8, 2, 8), DEVICE)
    dp, mp = ("x", "z", "core"), "y"
    placed = (P(dp, mp), P(dp, mp), P(mp, dp), P(mp, dp), P(), P(mp, dp))
    return jax.shard_map(
        on_device,
        mesh=inner,
        in_specs=placed,
        out_specs=(P(mp, dp), P(mp, dp), P(), P(mp, dp), P(mp, None), P(), P()),
        check_vma=False,
    )
```

```python
import functools

import jax
import jax.numpy as jnp
from jax import lax
from jax.experimental import pallas as pl
from jax.experimental.pallas import tpu as pltpu
from jax.sharding import Mesh, PartitionSpec as P

EPSILON = 1e-06
BETA_ONE = 0.9
BETA_TWO = 0.999
LEARN_RATE = 0.001
DECAY_RATE = 0.1
ADAM_EPSILON = 1e-08

F32 = jnp.float32
BF16 = jnp.bfloat16
LANES = 128
HALF = LANES // 2
TOP_ROWS = 16
TILE = 512
DEVICE = ("x", "z", "core", "y")
SMEM = pl.BlockSpec(memory_space=pltpu.SMEM)
VMEM = pl.BlockSpec(memory_space=pltpu.VMEM)
MIB = 1024 * 1024


def grant(size):
    return pltpu.CompilerParams(vmem_limit_bytes=size * MIB)


def fold(middle, odd):
    rows = middle.shape[0] // 2
    upper, lower = middle[:rows], pltpu.roll(middle[rows:], HALF, 1)
    left = lax.broadcasted_iota(jnp.int32, upper.shape, 1) < HALF
    return jnp.where(left, lower, upper) if odd else jnp.where(left, upper, lower)


def unfold(even_tail, odd_tail):
    left = lax.broadcasted_iota(jnp.int32, even_tail.shape, 1) < HALF
    upper = jnp.where(left, even_tail, odd_tail)
    lower = pltpu.roll(jnp.where(left, odd_tail, even_tail), HALF, 1)
    return jnp.concatenate([upper, lower], 0)


def largest(value):
    return jnp.max(jnp.max(jnp.abs(value), axis=1, keepdims=True), axis=0, keepdims=True)


def magnitude(value, best):
    top = jnp.max(jnp.abs(value).reshape(-1, 8, value.shape[1]), axis=0)
    for start in range(0, value.shape[1], LANES):
        part = top[:, start : start + LANES]
        best = part if best is None else jnp.maximum(best, part)
    return best


def split(top):
    high = top.astype(BF16).astype(F32)
    middle = (top - high).astype(BF16).astype(F32)
    low = top - high - middle
    row = lax.broadcasted_iota(jnp.int32, top.shape, 0)
    high = jnp.where(row < 4, high, pltpu.roll(low, 4, 0))
    return jnp.concatenate([high, middle], 0).astype(BF16)


def joined(spread):
    spread = spread.astype(F32)
    return spread[:8] + spread[8:] + pltpu.roll(spread[:8], 4, 0)


ABOVE = (((4, 0), (-1, 3)), ((2, -2), (-3, 1)))


def block_of(core, odd, which, y):
    place = (core + odd) % 2 + 2 * which
    if isinstance(core, int):
        above = ABOVE[core][odd][which]
    else:
        above = jnp.where(core == 0, ABOVE[0][odd][which], ABOVE[1][odd][which])
    return (place + y // 2) % 4, (y + above + 8) % 8


def slot_of(feature, y):
    near = feature // 2 if feature % 2 == 0 else 7 - feature // 2
    return (near + 4 * (y % 2)) % 8


def core_and_y(place_ref):
    return place_ref[0] // 8, place_ref[0] % 8


def multiply(grads, activations_ref, best, *outs):
    grads = jnp.concatenate(grads, 0)
    rows = outs[0].shape[1]
    for start in range(0, activations_ref.shape[1], TILE):
        where = slice(start, start + TILE)
        value = jnp.dot(grads, activations_ref[:, where], preferred_element_type=F32)
        first = 0
        for out_ref in outs:
            for block in range(out_ref.shape[0]):
                out_ref[block, :, where] = value[first : first + rows].astype(out_ref.dtype)
                first += rows
        best = magnitude(value, best)
    return best


def multiply_even(place_ref, grads_ref, activations_ref, other_out, own_out, top_out):
    core, y = core_and_y(place_ref)
    grads = []
    for adder in (1 - core, core):
        for which in range(2):
            grads.append(grads_ref[block_of(adder, 0, which, y)[1] // 2])
    top_out[...] = multiply(grads, activations_ref, None, other_out, own_out)


def multiply_odd(of_other, place_ref, first_ref, second_ref, activations_ref, top_ref, out_ref, top_out):
    core, y = core_and_y(place_ref)
    grads = []
    for which in range(2):
        block = block_of(1 - core if of_other else core, 1, which, y)[1] // 2
        grads.append(jnp.where(block // 2 == core, first_ref[block % 2], second_ref[block % 2]))
    top_out[...] = multiply(grads, activations_ref, top_ref[...], out_ref)


def add_cores(place_ref, own_even_ref, own_odd_ref, other_even_ref, other_odd_ref, out_ref):
    core, y = core_and_y(place_ref)
    for odd, own_ref, other_ref in ((0, own_even_ref, other_even_ref), (1, own_odd_ref, other_odd_ref)):
        for which in range(2):
            x = block_of(core, odd, which, y)[0]
            out_ref[x] = (own_ref[which] + other_ref[which].astype(F32)).astype(BF16)


def add_and_cut(place_ref, parts_ref, out_ref):
    y = core_and_y(place_ref)[1]
    rows = parts_ref.shape[1]

    def total(tile):
        where = slice(tile * LANES, (tile + 1) * LANES)
        value = parts_ref[0, :, where].astype(F32)
        for part in range(1, parts_ref.shape[0]):
            value += parts_ref[part, :, where].astype(F32)
        return value

    for pair in range(out_ref.shape[0] // 2):
        middle = total(3 * pair + 1)
        for odd in range(2):
            slot = slot_of(2 * pair + odd, y)
            out_ref[slot, :rows] = total(3 * pair + 2 * odd).astype(BF16)
            out_ref[slot, rows:] = fold(middle, odd).astype(BF16)


def adam_step(
    devices, place_ref, range_ref, summed_ref, top_ref, master_ref, moment_ref, second_ref,
    master_out, second_out, moment_out, sent_out,
):
    rows = master_ref.shape[0]
    is_even = core_and_y(place_ref)[0] == 0
    own, tail = summed_ref[:rows], summed_ref[rows:]
    middle = unfold(tail, tail)
    gradient = jnp.where(
        is_even,
        jnp.concatenate([own, middle[:, :HALF]], 1),
        jnp.concatenate([middle[:, HALF:], own], 1),
    ) / devices
    moment = (
        BETA_ONE * (moment_ref[...].astype(F32) * range_ref[0]) + (1.0 - BETA_ONE) * gradient
    )
    second_new = BETA_TWO * second_ref[...] + (1.0 - BETA_TWO) * gradient * gradient
    master = master_ref[...]
    master_new = master - LEARN_RATE * (
        moment / (jnp.sqrt(second_new) + ADAM_EPSILON) + DECAY_RATE * master
    )
    master_out[...] = master_new
    second_out[...] = second_new
    moment_out[...] = moment
    own = jnp.where(is_even, master_new[:, :LANES], master_new[:, HALF:]).astype(BF16)
    middle = jnp.concatenate([master_new[:, LANES:], master_new[:, :HALF]], 1)
    tail = jnp.where(is_even, fold(middle, False), fold(middle, True)).astype(BF16)
    row = lax.broadcasted_iota(jnp.int32, (8, LANES), 0)
    tops = (largest(top_ref[...]), largest(moment), largest(master_new))
    spread = split(jnp.where(row == 0, tops[0], jnp.where(row == 1, tops[1], tops[2])))
    for copy in range(sent_out.shape[0]):
        sent_out[copy, :rows] = own
        sent_out[copy, rows : rows + rows // 2] = tail
        sent_out[copy, rows + rows // 2 :] = spread


def join_blocks(held_ref, out_ref):
    packed = held_ref.shape[1] - TOP_ROWS
    best = None
    for z in range(held_ref.shape[0]):
        out_ref[z * packed : (z + 1) * packed] = held_ref[z, :packed]
        top = joined(held_ref[z, packed:])
        best = top if best is None else jnp.maximum(best, top)
    out_ref[held_ref.shape[0] * packed :] = split(best)


def join_tops(held_ref, out_ref):
    packed = held_ref.shape[1] - TOP_ROWS
    best = joined(held_ref[0, packed:])
    for x in range(1, held_ref.shape[0]):
        best = jnp.maximum(best, joined(held_ref[x, packed:]))
    for copy in range(out_ref.shape[0]):
        out_ref[copy] = best


def scale_weights(
    place_ref, tops_ref, own_ref, other_ref, moment_ref,
    weight_out, moment_out, moment_span_out, weight_span_out, grad_span_out, span_ref,
):
    rows = weight_out.shape[0]
    packed = rows + rows // 2
    step = pl.program_id(0)
    is_even = core_and_y(place_ref)[0] == 0

    @pl.when(step == 0)
    def _():
        best = tops_ref[0]
        for place in range(1, tops_ref.shape[0]):
            best = jnp.maximum(best, tops_ref[place])
        spans = best + EPSILON
        span_ref[...] = spans
        moment_out[...] = (moment_ref[...] / largest(spans[1:2])).astype(BF16)
        grad_span_out[0] = jnp.max(spans[0:1])
        moment_span_out[0] = jnp.max(spans[1:2])
        weight_span_out[0] = jnp.max(spans[2:3])

    scale = 1.0 / span_ref[2:3]
    for place in range((own_ref.shape[1] - TOP_ROWS) // packed):
        where = slice(place * packed, (place + 1) * packed)
        own = own_ref[step, where].astype(F32) * scale
        other = other_ref[step, where].astype(F32) * scale
        even, odd = jnp.where(is_even, own, other), jnp.where(is_even, other, own)
        start = 3 * LANES * place
        weight_out[:, start : start + LANES] = even[:rows].astype(BF16)
        weight_out[:, start + LANES : start + 2 * LANES] = unfold(even[rows:], odd[rows:]).astype(BF16)
        weight_out[:, start + 2 * LANES : start + 3 * LANES] = odd[:rows].astype(BF16)


def on_device(activations, output_grads, master, moment_q, moment_range, second_moment):
    xs, zs, cores, ys = (lax.axis_size(name) for name in DEVICE)
    rows, width = master.shape
    packed = rows + rows // 2
    sent_rows = packed + TOP_ROWS
    place = lax.axis_index(("core", "y")).reshape(1)
    output_grads, place = lax.optimization_barrier((output_grads, place))
    swap = [(0, 1), (1, 0)]

    tokens, columns = output_grads.shape
    every_second = [list(range(first, ys, 2)) for first in range(2)]
    even = lax.all_gather(output_grads.T, "y", axis_index_groups=every_second)
    half = ys // 4
    down = [(y, (y - 1) % ys) for y in range(ys)]
    up = [(y, (y + 1) % ys) for y in range(ys)]

    def both(first, second):
        return [(own, to) for own, to in first] + [(ys + own, ys + to) for own, to in second]

    core = lax.axis_index("core")
    first = lax.dynamic_slice_in_dim(even, core * half, half, 0)
    second = lax.dynamic_slice_in_dim(even, (1 - core) * half, half, 0)
    first = lax.ppermute(first, ("core", "y"), both(down, up))
    second = lax.ppermute(second, ("core", "y"), both(up, down))

    def product(dtype):
        return jax.ShapeDtypeStruct((2, columns, activations.shape[1]), dtype)

    top_shape = jax.ShapeDtypeStruct((8, LANES), F32)
    to_other_even, own_even, top = pl.pallas_call(
        multiply_even,
        out_shape=(product(BF16), product(F32), top_shape),
        in_specs=[SMEM, VMEM, VMEM],
        out_specs=(VMEM,) * 3,
        compiler_params=grant(8),
    )(place, even, activations)
    to_other_odd, top = pl.pallas_call(
        functools.partial(multiply_odd, True),
        out_shape=(product(BF16), top_shape),
        in_specs=[SMEM] + [VMEM] * 4,
        out_specs=(VMEM, VMEM),
        compiler_params=grant(8),
    )(place, first, second, activations, top)
    own_odd, top = pl.pallas_call(
        functools.partial(multiply_odd, False),
        out_shape=(product(F32), top_shape),
        in_specs=[SMEM] + [VMEM] * 4,
        out_specs=(VMEM, VMEM),
        compiler_params=grant(8),
    )(place, first, second, activations, top)

    other_even = lax.ppermute(to_other_even, "core", swap)
    other_odd = lax.ppermute(to_other_odd, "core", swap)
    value = pl.pallas_call(
        add_cores,
        out_shape=jax.ShapeDtypeStruct((xs, rows, activations.shape[1]), BF16),
        in_specs=[SMEM] + [VMEM] * 4,
        out_specs=VMEM,
        compiler_params=grant(10),
    )(place, own_even, own_odd, other_even, other_odd)
    value = lax.all_to_all(value, "x", 0, 0, tiled=True)
    value = pl.pallas_call(
        add_and_cut,
        out_shape=jax.ShapeDtypeStruct((zs, packed, LANES), BF16),
        in_specs=[SMEM, VMEM],
        out_specs=VMEM,
        compiler_params=grant(4),
    )(place, value)
    value = lax.all_to_all(value, "z", 0, 0, tiled=True)
    value = jnp.sum(value.astype(F32), axis=0)
    route = []
    for half in range(cores):
        for odd in range(2):
            for which in range(2):
                for y in range(ys):
                    x, column = block_of(half, odd, which, y)
                    for feature in range(zs):
                        source = ((x * zs + slot_of(feature, y)) * cores + half) * ys + y
                        route.append((source, (y * zs + feature) * ys + column))
    value = lax.ppermute(value, DEVICE, route)

    block = jax.ShapeDtypeStruct((rows, width), F32)
    master_new, second_new, moment, held = pl.pallas_call(
        functools.partial(adam_step, xs * zs * cores),
        out_shape=(block, block, block, jax.ShapeDtypeStruct((zs, sent_rows, LANES), BF16)),
        in_specs=[SMEM, SMEM] + [VMEM] * 5,
        out_specs=(VMEM,) * 4,
        compiler_params=grant(4),
    )(place, moment_range, value, top, master, moment_q, second_moment)

    held = lax.all_to_all(held, "z", 0, 0, tiled=True)
    held = pl.pallas_call(
        join_blocks,
        out_shape=jax.ShapeDtypeStruct((zs * packed + TOP_ROWS, LANES), BF16),
        in_specs=[VMEM],
        out_specs=VMEM,
        compiler_params=grant(4),
    )(held)
    held = lax.all_gather(held, "x")
    other = lax.ppermute(held, "core", swap)
    tops = pl.pallas_call(
        join_tops,
        out_shape=jax.ShapeDtypeStruct((cores * ys, 8, LANES), F32),
        in_specs=[VMEM],
        out_specs=VMEM,
        compiler_params=grant(4),
    )(held)
    tops = lax.all_to_all(tops, ("core", "y"), 0, 0, tiled=True)

    one = jax.ShapeDtypeStruct((1,), F32)
    weight_q, moment_q_new, moment_span, weight_span, grad_span = pl.pallas_call(
        scale_weights,
        grid=(xs,),
        out_shape=(
            jax.ShapeDtypeStruct((rows, width * xs * zs * cores), BF16),
            jax.ShapeDtypeStruct((rows, width), BF16),
            one,
            one,
            one,
        ),
        in_specs=[SMEM, VMEM, VMEM, VMEM, VMEM],
        out_specs=(
            pl.BlockSpec((rows, width * zs * cores), lambda i: (0, i)),
            VMEM,
            SMEM,
            SMEM,
            SMEM,
        ),
        scratch_shapes=[pltpu.VMEM((8, LANES), F32)],
        compiler_params=grant(8),
    )(place, tops, held, other, moment)
    return master_new, moment_q_new, moment_span, second_new, weight_q, weight_span, grad_span


def solution(mesh):
    inner = Mesh(mesh.devices.reshape(4, 8, 2, 8), DEVICE)
    dp, mp = ("x", "z", "core"), "y"
    placed = (P(dp, mp), P(dp, mp), P(mp, dp), P(mp, dp), P(), P(mp, dp))
    return jax.shard_map(
        on_device,
        mesh=inner,
        in_specs=placed,
        out_specs=(P(mp, dp), P(mp, dp), P(), P(mp, dp), P(mp, None), P(), P()),
        check_vma=False,
    )
```

```python
import functools

import jax
import jax.numpy as jnp
from jax import lax
from jax.experimental import pallas as pl
from jax.experimental.pallas import tpu as pltpu
from jax.sharding import Mesh, PartitionSpec as P

EPSILON = 1e-06
BETA_ONE = 0.9
BETA_TWO = 0.999
LEARN_RATE = 0.001
DECAY_RATE = 0.1
ADAM_EPSILON = 1e-08

F32 = jnp.float32
BF16 = jnp.bfloat16
LANES = 128
HALF = LANES // 2
TOP_ROWS = 16
TILE = 512
DEVICE = ("x", "z", "core", "y")
SMEM = pl.BlockSpec(memory_space=pltpu.SMEM)
VMEM = pl.BlockSpec(memory_space=pltpu.VMEM)
MIB = 1024 * 1024


def grant(size):
    return pltpu.CompilerParams(vmem_limit_bytes=size * MIB)


def fold(middle, odd):
    rows = middle.shape[0] // 2
    upper, lower = middle[:rows], pltpu.roll(middle[rows:], HALF, 1)
    left = lax.broadcasted_iota(jnp.int32, upper.shape, 1) < HALF
    return jnp.where(left, lower, upper) if odd else jnp.where(left, upper, lower)


def unfold(even_tail, odd_tail):
    left = lax.broadcasted_iota(jnp.int32, even_tail.shape, 1) < HALF
    upper = jnp.where(left, even_tail, odd_tail)
    lower = pltpu.roll(jnp.where(left, odd_tail, even_tail), HALF, 1)
    return jnp.concatenate([upper, lower], 0)


def largest(value):
    return jnp.max(jnp.max(jnp.abs(value), axis=1, keepdims=True), axis=0, keepdims=True)


def magnitude(value, best):
    top = jnp.max(jnp.abs(value).reshape(-1, 8, value.shape[1]), axis=0)
    for start in range(0, value.shape[1], LANES):
        part = top[:, start : start + LANES]
        best = part if best is None else jnp.maximum(best, part)
    return best


def split(top):
    high = top.astype(BF16).astype(F32)
    middle = (top - high).astype(BF16).astype(F32)
    low = top - high - middle
    row = lax.broadcasted_iota(jnp.int32, top.shape, 0)
    high = jnp.where(row < 4, high, pltpu.roll(low, 4, 0))
    return jnp.concatenate([high, middle], 0).astype(BF16)


def joined(spread):
    spread = spread.astype(F32)
    return spread[:8] + spread[8:] + pltpu.roll(spread[:8], 4, 0)


ABOVE = (((4, 0), (-1, 3)), ((2, -2), (-3, 1)))


def block_of(core, odd, which, y):
    place = (core + odd) % 2 + 2 * which
    if isinstance(core, int):
        above = ABOVE[core][odd][which]
    else:
        above = jnp.where(core == 0, ABOVE[0][odd][which], ABOVE[1][odd][which])
    return (place + y // 2) % 4, (y + above + 8) % 8


def slot_of(feature, y):
    near = feature // 2 if feature % 2 == 0 else 7 - feature // 2
    return (near + 4 * (y % 2)) % 8


def core_and_y(place_ref):
    return place_ref[0] // 8, place_ref[0] % 8


def multiply(grads, activations_ref, best, *outs):
    grads = jnp.concatenate(grads, 0)
    rows = outs[0].shape[1]
    for start in range(0, activations_ref.shape[1], TILE):
        where = slice(start, start + TILE)
        value = jnp.dot(grads, activations_ref[:, where], preferred_element_type=F32)
        first = 0
        for out_ref in outs:
            for block in range(out_ref.shape[0]):
                out_ref[block, :, where] = value[first : first + rows].astype(out_ref.dtype)
                first += rows
        best = magnitude(value, best)
    return best


def multiply_even(place_ref, grads_ref, activations_ref, other_out, own_out, top_out):
    core, y = core_and_y(place_ref)
    grads = []
    for adder in (1 - core, core):
        for which in range(2):
            grads.append(grads_ref[block_of(adder, 0, which, y)[1] // 2])
    top_out[...] = multiply(grads, activations_ref, None, other_out, own_out)


def multiply_odd(of_other, place_ref, low_ref, high_ref, activations_ref, top_ref, out_ref, top_out):
    core, y = core_and_y(place_ref)
    grads = []
    for which in range(2):
        block = block_of(1 - core if of_other else core, 1, which, y)[1] // 2
        grads.append(jnp.where(block < 2, low_ref[block % 2], high_ref[block % 2]))
    top_out[...] = multiply(grads, activations_ref, top_ref[...], out_ref)


def add_cores(place_ref, own_even_ref, own_odd_ref, other_even_ref, other_odd_ref, out_ref):
    core, y = core_and_y(place_ref)
    for odd, own_ref, other_ref in ((0, own_even_ref, other_even_ref), (1, own_odd_ref, other_odd_ref)):
        for which in range(2):
            x = block_of(core, odd, which, y)[0]
            out_ref[x] = (own_ref[which] + other_ref[which]).astype(BF16)


def add_and_cut(place_ref, parts_ref, out_ref):
    y = core_and_y(place_ref)[1]
    rows = parts_ref.shape[1]

    def total(tile):
        where = slice(tile * LANES, (tile + 1) * LANES)
        value = parts_ref[0, :, where].astype(F32)
        for part in range(1, parts_ref.shape[0]):
            value += parts_ref[part, :, where].astype(F32)
        return value

    for pair in range(out_ref.shape[0] // 2):
        middle = total(3 * pair + 1)
        for odd in range(2):
            slot = slot_of(2 * pair + odd, y)
            out_ref[slot, :rows] = total(3 * pair + 2 * odd)
            out_ref[slot, rows:] = fold(middle, odd)


def adam_step(
    devices, place_ref, range_ref, summed_ref, top_ref, master_ref, moment_ref, second_ref,
    master_out, second_out, moment_out, sent_out,
):
    rows = master_ref.shape[0]
    is_even = core_and_y(place_ref)[0] == 0
    own, tail = summed_ref[:rows], summed_ref[rows:]
    middle = unfold(tail, tail)
    gradient = jnp.where(
        is_even,
        jnp.concatenate([own, middle[:, :HALF]], 1),
        jnp.concatenate([middle[:, HALF:], own], 1),
    ) / devices
    moment = (
        BETA_ONE * (moment_ref[...].astype(F32) * range_ref[0]) + (1.0 - BETA_ONE) * gradient
    )
    second_new = BETA_TWO * second_ref[...] + (1.0 - BETA_TWO) * gradient * gradient
    master = master_ref[...]
    master_new = master - LEARN_RATE * (
        moment / (jnp.sqrt(second_new) + ADAM_EPSILON) + DECAY_RATE * master
    )
    master_out[...] = master_new
    second_out[...] = second_new
    moment_out[...] = moment
    own = jnp.where(is_even, master_new[:, :LANES], master_new[:, HALF:]).astype(BF16)
    middle = jnp.concatenate([master_new[:, LANES:], master_new[:, :HALF]], 1)
    tail = jnp.where(is_even, fold(middle, False), fold(middle, True)).astype(BF16)
    row = lax.broadcasted_iota(jnp.int32, (8, LANES), 0)
    tops = (largest(top_ref[...]), largest(moment), largest(master_new))
    spread = split(jnp.where(row == 0, tops[0], jnp.where(row == 1, tops[1], tops[2])))
    for copy in range(sent_out.shape[0]):
        sent_out[copy, :rows] = own
        sent_out[copy, rows : rows + rows // 2] = tail
        sent_out[copy, rows + rows // 2 :] = spread


def join_blocks(held_ref, out_ref):
    packed = held_ref.shape[1] - TOP_ROWS
    best = None
    for z in range(held_ref.shape[0]):
        out_ref[z * packed : (z + 1) * packed] = held_ref[z, :packed]
        top = joined(held_ref[z, packed:])
        best = top if best is None else jnp.maximum(best, top)
    out_ref[held_ref.shape[0] * packed :] = split(best)


def join_tops(held_ref, out_ref):
    packed = held_ref.shape[1] - TOP_ROWS
    best = joined(held_ref[0, packed:])
    for x in range(1, held_ref.shape[0]):
        best = jnp.maximum(best, joined(held_ref[x, packed:]))
    for copy in range(out_ref.shape[0]):
        out_ref[copy] = best


def scale_weights(
    place_ref, tops_ref, own_ref, other_ref, moment_ref,
    weight_out, moment_out, moment_span_out, weight_span_out, grad_span_out, span_ref,
):
    rows = weight_out.shape[0]
    packed = rows + rows // 2
    step = pl.program_id(0)
    is_even = core_and_y(place_ref)[0] == 0

    @pl.when(step == 0)
    def _():
        best = tops_ref[0]
        for place in range(1, tops_ref.shape[0]):
            best = jnp.maximum(best, tops_ref[place])
        spans = best + EPSILON
        span_ref[...] = spans
        moment_out[...] = (moment_ref[...] / largest(spans[1:2])).astype(BF16)
        grad_span_out[0] = jnp.max(spans[0:1])
        moment_span_out[0] = jnp.max(spans[1:2])
        weight_span_out[0] = jnp.max(spans[2:3])

    scale = 1.0 / span_ref[2:3]
    for place in range((own_ref.shape[1] - TOP_ROWS) // packed):
        where = slice(place * packed, (place + 1) * packed)
        own = own_ref[step, where].astype(F32) * scale
        other = other_ref[step, where].astype(F32) * scale
        even, odd = jnp.where(is_even, own, other), jnp.where(is_even, other, own)
        start = 3 * LANES * place
        weight_out[:, start : start + LANES] = even[:rows].astype(BF16)
        weight_out[:, start + LANES : start + 2 * LANES] = unfold(even[rows:], odd[rows:]).astype(BF16)
        weight_out[:, start + 2 * LANES : start + 3 * LANES] = odd[:rows].astype(BF16)


def on_device(activations, output_grads, master, moment_q, moment_range, second_moment):
    xs, zs, cores, ys = (lax.axis_size(name) for name in DEVICE)
    rows, width = master.shape
    packed = rows + rows // 2
    sent_rows = packed + TOP_ROWS
    place = lax.axis_index(("core", "y")).reshape(1)
    output_grads, place = lax.optimization_barrier((output_grads, place))
    swap = [(0, 1), (1, 0)]

    tokens, columns = output_grads.shape
    every_second = [list(range(first, ys, 2)) for first in range(2)]
    even = lax.all_gather(output_grads.T, "y", axis_index_groups=every_second)
    low = lax.ppermute(even[: ys // 4], "y", [(y, (y - 1) % ys) for y in range(ys)])
    high = lax.ppermute(even[ys // 4 :], "y", [(y, (y + 1) % ys) for y in range(ys)])

    def product(dtype):
        return jax.ShapeDtypeStruct((2, columns, activations.shape[1]), dtype)

    top_shape = jax.ShapeDtypeStruct((8, LANES), F32)
    to_other_even, own_even, top = pl.pallas_call(
        multiply_even,
        out_shape=(product(F32), product(F32), top_shape),
        in_specs=[SMEM, VMEM, VMEM],
        out_specs=(VMEM,) * 3,
        compiler_params=grant(14),
    )(place, even, activations)
    to_other_odd, top = pl.pallas_call(
        functools.partial(multiply_odd, True),
        out_shape=(product(F32), top_shape),
        in_specs=[SMEM] + [VMEM] * 4,
        out_specs=(VMEM, VMEM),
        compiler_params=grant(14),
    )(place, low, high, activations, top)
    own_odd, top = pl.pallas_call(
        functools.partial(multiply_odd, False),
        out_shape=(product(F32), top_shape),
        in_specs=[SMEM] + [VMEM] * 4,
        out_specs=(VMEM, VMEM),
        compiler_params=grant(14),
    )(place, low, high, activations, top)

    other_even = lax.ppermute(to_other_even, "core", swap)
    other_odd = lax.ppermute(to_other_odd, "core", swap)
    value = pl.pallas_call(
        add_cores,
        out_shape=jax.ShapeDtypeStruct((xs, rows, activations.shape[1]), BF16),
        in_specs=[SMEM] + [VMEM] * 4,
        out_specs=VMEM,
        compiler_params=grant(10),
    )(place, own_even, own_odd, other_even, other_odd)
    value = lax.all_to_all(value, "x", 0, 0, tiled=True)
    value = pl.pallas_call(
        add_and_cut,
        out_shape=jax.ShapeDtypeStruct((zs, packed, LANES), F32),
        in_specs=[SMEM, VMEM],
        out_specs=VMEM,
        compiler_params=grant(4),
    )(place, value)
    value = lax.all_to_all(value, "z", 0, 0, tiled=True)
    value = jnp.sum(value, axis=0)
    route = []
    for half in range(cores):
        for odd in range(2):
            for which in range(2):
                for y in range(ys):
                    x, column = block_of(half, odd, which, y)
                    for feature in range(zs):
                        source = ((x * zs + slot_of(feature, y)) * cores + half) * ys + y
                        route.append((source, (y * zs + feature) * ys + column))
    value = lax.ppermute(value, DEVICE, route)

    block = jax.ShapeDtypeStruct((rows, width), F32)
    master_new, second_new, moment, held = pl.pallas_call(
        functools.partial(adam_step, xs * zs * cores),
        out_shape=(block, block, block, jax.ShapeDtypeStruct((zs, sent_rows, LANES), BF16)),
        in_specs=[SMEM, SMEM] + [VMEM] * 5,
        out_specs=(VMEM,) * 4,
        compiler_params=grant(4),
    )(place, moment_range, value, top, master, moment_q, second_moment)

    held = lax.all_to_all(held, "z", 0, 0, tiled=True)
    held = pl.pallas_call(
        join_blocks,
        out_shape=jax.ShapeDtypeStruct((zs * packed + TOP_ROWS, LANES), BF16),
        in_specs=[VMEM],
        out_specs=VMEM,
        compiler_params=grant(4),
    )(held)
    held = lax.all_gather(held, "x")
    other = lax.ppermute(held, "core", swap)
    tops = pl.pallas_call(
        join_tops,
        out_shape=jax.ShapeDtypeStruct((cores * ys, 8, LANES), F32),
        in_specs=[VMEM],
        out_specs=VMEM,
        compiler_params=grant(4),
    )(held)
    tops = lax.all_to_all(tops, ("core", "y"), 0, 0, tiled=True)

    one = jax.ShapeDtypeStruct((1,), F32)
    weight_q, moment_q_new, moment_span, weight_span, grad_span = pl.pallas_call(
        scale_weights,
        grid=(xs,),
        out_shape=(
            jax.ShapeDtypeStruct((rows, width * xs * zs * cores), BF16),
            jax.ShapeDtypeStruct((rows, width), BF16),
            one,
            one,
            one,
        ),
        in_specs=[SMEM, VMEM, VMEM, VMEM, VMEM],
        out_specs=(
            pl.BlockSpec((rows, width * zs * cores), lambda i: (0, i)),
            VMEM,
            SMEM,
            SMEM,
            SMEM,
        ),
        scratch_shapes=[pltpu.VMEM((8, LANES), F32)],
        compiler_params=grant(8),
    )(place, tops, held, other, moment)
    return master_new, moment_q_new, moment_span, second_new, weight_q, weight_span, grad_span


def solution(mesh):
    inner = Mesh(mesh.devices.reshape(4, 8, 2, 8), DEVICE)
    dp, mp = ("x", "z", "core"), "y"
    placed = (P(dp, mp), P(dp, mp), P(mp, dp), P(mp, dp), P(), P(mp, dp))
    return jax.shard_map(
        on_device,
        mesh=inner,
        in_specs=placed,
        out_specs=(P(mp, dp), P(mp, dp), P(), P(mp, dp), P(mp, None), P(), P()),
        check_vma=False,
    )
```

```python
import functools

import jax
import jax.numpy as jnp
from jax import lax
from jax.experimental import pallas as pl
from jax.experimental.pallas import tpu as pltpu
from jax.sharding import Mesh, PartitionSpec as P

EPSILON = 1e-06
BETA_ONE = 0.9
BETA_TWO = 0.999
LEARN_RATE = 0.001
DECAY_RATE = 0.1
ADAM_EPSILON = 1e-08

F32 = jnp.float32
BF16 = jnp.bfloat16
LANES = 128
HALF = LANES // 2
TOP_ROWS = 16
TILE = 512
DEVICE = ("x", "z", "core", "y")
SMEM = pl.BlockSpec(memory_space=pltpu.SMEM)
VMEM = pl.BlockSpec(memory_space=pltpu.VMEM)
MIB = 1024 * 1024


def grant(size):
    return pltpu.CompilerParams(vmem_limit_bytes=size * MIB)


def fold(middle, odd):
    rows = middle.shape[0] // 2
    upper, lower = middle[:rows], pltpu.roll(middle[rows:], HALF, 1)
    left = lax.broadcasted_iota(jnp.int32, upper.shape, 1) < HALF
    return jnp.where(left, lower, upper) if odd else jnp.where(left, upper, lower)


def unfold(even_tail, odd_tail):
    left = lax.broadcasted_iota(jnp.int32, even_tail.shape, 1) < HALF
    upper = jnp.where(left, even_tail, odd_tail)
    lower = pltpu.roll(jnp.where(left, odd_tail, even_tail), HALF, 1)
    return jnp.concatenate([upper, lower], 0)


def largest(value):
    return jnp.max(jnp.max(jnp.abs(value), axis=1, keepdims=True), axis=0, keepdims=True)


def magnitude(value, best):
    top = jnp.max(jnp.abs(value).reshape(-1, 8, value.shape[1]), axis=0)
    for start in range(0, value.shape[1], LANES):
        part = top[:, start : start + LANES]
        best = part if best is None else jnp.maximum(best, part)
    return best


def split(top):
    high = top.astype(BF16).astype(F32)
    middle = (top - high).astype(BF16).astype(F32)
    low = top - high - middle
    row = lax.broadcasted_iota(jnp.int32, top.shape, 0)
    high = jnp.where(row < 4, high, pltpu.roll(low, 4, 0))
    return jnp.concatenate([high, middle], 0).astype(BF16)


def joined(spread):
    spread = spread.astype(F32)
    return spread[:8] + spread[8:] + pltpu.roll(spread[:8], 4, 0)


ABOVE = (((4, 0), (-1, 3)), ((2, -2), (-3, 1)))


def block_of(core, odd, which, y):
    place = (core + odd) % 2 + 2 * which
    if isinstance(core, int):
        above = ABOVE[core][odd][which]
    else:
        above = jnp.where(core == 0, ABOVE[0][odd][which], ABOVE[1][odd][which])
    return (place + y // 2) % 4, (y + above + 8) % 8


def slot_of(feature, y):
    near = feature // 2 if feature % 2 == 0 else 4 + (feature // 2 + 2) % 4
    return (near + 4 * (y % 2)) % 8


def core_and_y(place_ref):
    return place_ref[0] // 8, place_ref[0] % 8


def multiply(grads, activations_ref, best, *outs):
    grads = jnp.concatenate(grads, 0)
    rows = outs[0].shape[1]
    for start in range(0, activations_ref.shape[1], TILE):
        where = slice(start, start + TILE)
        value = jnp.dot(grads, activations_ref[:, where], preferred_element_type=F32)
        first = 0
        for out_ref in outs:
            for block in range(out_ref.shape[0]):
                out_ref[block, :, where] = value[first : first + rows].astype(out_ref.dtype)
                first += rows
        best = magnitude(value, best)
    return best


def multiply_even(place_ref, grads_ref, activations_ref, other_out, own_out, top_out):
    core, y = core_and_y(place_ref)
    grads = []
    for adder in (1 - core, core):
        for which in range(2):
            grads.append(grads_ref[block_of(adder, 0, which, y)[1] // 2])
    top_out[...] = multiply(grads, activations_ref, None, other_out, own_out)


def multiply_odd(of_other, place_ref, low_ref, high_ref, activations_ref, top_ref, out_ref, top_out):
    core, y = core_and_y(place_ref)
    grads = []
    for which in range(2):
        block = block_of(1 - core if of_other else core, 1, which, y)[1] // 2
        grads.append(jnp.where(block < 2, low_ref[block % 2], high_ref[block % 2]))
    top_out[...] = multiply(grads, activations_ref, top_ref[...], out_ref)


def add_cores(place_ref, own_even_ref, own_odd_ref, other_even_ref, other_odd_ref, out_ref):
    core, y = core_and_y(place_ref)
    for odd, own_ref, other_ref in ((0, own_even_ref, other_even_ref), (1, own_odd_ref, other_odd_ref)):
        for which in range(2):
            x = block_of(core, odd, which, y)[0]
            out_ref[x] = (own_ref[which] + other_ref[which]).astype(BF16)


def add_and_cut(place_ref, parts_ref, out_ref):
    y = core_and_y(place_ref)[1]
    rows = parts_ref.shape[1]

    def total(tile):
        where = slice(tile * LANES, (tile + 1) * LANES)
        value = parts_ref[0, :, where].astype(F32)
        for part in range(1, parts_ref.shape[0]):
            value += parts_ref[part, :, where].astype(F32)
        return value

    for pair in range(out_ref.shape[0] // 2):
        middle = total(3 * pair + 1)
        for odd in range(2):
            slot = slot_of(2 * pair + odd, y)
            out_ref[slot, :rows] = total(3 * pair + 2 * odd)
            out_ref[slot, rows:] = fold(middle, odd)


def adam_step(
    devices, place_ref, range_ref, summed_ref, top_ref, master_ref, moment_ref, second_ref,
    master_out, second_out, moment_out, sent_out,
):
    rows = master_ref.shape[0]
    is_even = core_and_y(place_ref)[0] == 0
    own, tail = summed_ref[:rows], summed_ref[rows:]
    middle = unfold(tail, tail)
    gradient = jnp.where(
        is_even,
        jnp.concatenate([own, middle[:, :HALF]], 1),
        jnp.concatenate([middle[:, HALF:], own], 1),
    ) / devices
    moment = (
        BETA_ONE * (moment_ref[...].astype(F32) * range_ref[0]) + (1.0 - BETA_ONE) * gradient
    )
    second_new = BETA_TWO * second_ref[...] + (1.0 - BETA_TWO) * gradient * gradient
    master = master_ref[...]
    master_new = master - LEARN_RATE * (
        moment / (jnp.sqrt(second_new) + ADAM_EPSILON) + DECAY_RATE * master
    )
    master_out[...] = master_new
    second_out[...] = second_new
    moment_out[...] = moment
    own = jnp.where(is_even, master_new[:, :LANES], master_new[:, HALF:]).astype(BF16)
    middle = jnp.concatenate([master_new[:, LANES:], master_new[:, :HALF]], 1)
    tail = jnp.where(is_even, fold(middle, False), fold(middle, True)).astype(BF16)
    row = lax.broadcasted_iota(jnp.int32, (8, LANES), 0)
    tops = (largest(top_ref[...]), largest(moment), largest(master_new))
    spread = split(jnp.where(row == 0, tops[0], jnp.where(row == 1, tops[1], tops[2])))
    for copy in range(sent_out.shape[0]):
        sent_out[copy, :rows] = own
        sent_out[copy, rows : rows + rows // 2] = tail
        sent_out[copy, rows + rows // 2 :] = spread


def join_blocks(held_ref, out_ref):
    packed = held_ref.shape[1] - TOP_ROWS
    best = None
    for z in range(held_ref.shape[0]):
        out_ref[z * packed : (z + 1) * packed] = held_ref[z, :packed]
        top = joined(held_ref[z, packed:])
        best = top if best is None else jnp.maximum(best, top)
    out_ref[held_ref.shape[0] * packed :] = split(best)


def join_tops(held_ref, out_ref):
    packed = held_ref.shape[1] - TOP_ROWS
    best = joined(held_ref[0, packed:])
    for x in range(1, held_ref.shape[0]):
        best = jnp.maximum(best, joined(held_ref[x, packed:]))
    for copy in range(out_ref.shape[0]):
        out_ref[copy] = best


def scale_weights(
    place_ref, tops_ref, own_ref, other_ref, moment_ref,
    weight_out, moment_out, moment_span_out, weight_span_out, grad_span_out, span_ref,
):
    rows = weight_out.shape[0]
    packed = rows + rows // 2
    step = pl.program_id(0)
    is_even = core_and_y(place_ref)[0] == 0

    @pl.when(step == 0)
    def _():
        best = tops_ref[0]
        for place in range(1, tops_ref.shape[0]):
            best = jnp.maximum(best, tops_ref[place])
        spans = best + EPSILON
        span_ref[...] = spans
        moment_out[...] = (moment_ref[...] / largest(spans[1:2])).astype(BF16)
        grad_span_out[0] = jnp.max(spans[0:1])
        moment_span_out[0] = jnp.max(spans[1:2])
        weight_span_out[0] = jnp.max(spans[2:3])

    scale = 1.0 / span_ref[2:3]
    for place in range((own_ref.shape[1] - TOP_ROWS) // packed):
        where = slice(place * packed, (place + 1) * packed)
        own = own_ref[step, where].astype(F32) * scale
        other = other_ref[step, where].astype(F32) * scale
        even, odd = jnp.where(is_even, own, other), jnp.where(is_even, other, own)
        start = 3 * LANES * place
        weight_out[:, start : start + LANES] = even[:rows].astype(BF16)
        weight_out[:, start + LANES : start + 2 * LANES] = unfold(even[rows:], odd[rows:]).astype(BF16)
        weight_out[:, start + 2 * LANES : start + 3 * LANES] = odd[:rows].astype(BF16)


def on_device(activations, output_grads, master, moment_q, moment_range, second_moment):
    xs, zs, cores, ys = (lax.axis_size(name) for name in DEVICE)
    rows, width = master.shape
    packed = rows + rows // 2
    sent_rows = packed + TOP_ROWS
    place = lax.axis_index(("core", "y")).reshape(1)
    output_grads, place = lax.optimization_barrier((output_grads, place))
    swap = [(0, 1), (1, 0)]

    tokens, columns = output_grads.shape
    every_second = [list(range(first, ys, 2)) for first in range(2)]
    even = lax.all_gather(output_grads.T, "y", axis_index_groups=every_second)
    low = lax.ppermute(even[: ys // 4], "y", [(y, (y - 1) % ys) for y in range(ys)])
    high = lax.ppermute(even[ys // 4 :], "y", [(y, (y + 1) % ys) for y in range(ys)])

    def product(dtype):
        return jax.ShapeDtypeStruct((2, columns, activations.shape[1]), dtype)

    top_shape = jax.ShapeDtypeStruct((8, LANES), F32)
    to_other_even, own_even, top = pl.pallas_call(
        multiply_even,
        out_shape=(product(F32), product(F32), top_shape),
        in_specs=[SMEM, VMEM, VMEM],
        out_specs=(VMEM,) * 3,
        compiler_params=grant(14),
    )(place, even, activations)
    to_other_odd, top = pl.pallas_call(
        functools.partial(multiply_odd, True),
        out_shape=(product(F32), top_shape),
        in_specs=[SMEM] + [VMEM] * 4,
        out_specs=(VMEM, VMEM),
        compiler_params=grant(14),
    )(place, low, high, activations, top)
    own_odd, top = pl.pallas_call(
        functools.partial(multiply_odd, False),
        out_shape=(product(F32), top_shape),
        in_specs=[SMEM] + [VMEM] * 4,
        out_specs=(VMEM, VMEM),
        compiler_params=grant(14),
    )(place, low, high, activations, top)

    other_even = lax.ppermute(to_other_even, "core", swap)
    other_odd = lax.ppermute(to_other_odd, "core", swap)
    value = pl.pallas_call(
        add_cores,
        out_shape=jax.ShapeDtypeStruct((xs, rows, activations.shape[1]), BF16),
        in_specs=[SMEM] + [VMEM] * 4,
        out_specs=VMEM,
        compiler_params=grant(10),
    )(place, own_even, own_odd, other_even, other_odd)
    value = lax.all_to_all(value, "x", 0, 0, tiled=True)
    value = pl.pallas_call(
        add_and_cut,
        out_shape=jax.ShapeDtypeStruct((zs, packed, LANES), F32),
        in_specs=[SMEM, VMEM],
        out_specs=VMEM,
        compiler_params=grant(4),
    )(place, value)
    value = lax.all_to_all(value, "z", 0, 0, tiled=True)
    value = jnp.sum(value, axis=0)
    route = []
    for half in range(cores):
        for odd in range(2):
            for which in range(2):
                for y in range(ys):
                    x, column = block_of(half, odd, which, y)
                    for feature in range(zs):
                        source = ((x * zs + slot_of(feature, y)) * cores + half) * ys + y
                        route.append((source, (y * zs + feature) * ys + column))
    value = lax.ppermute(value, DEVICE, route)

    block = jax.ShapeDtypeStruct((rows, width), F32)
    master_new, second_new, moment, held = pl.pallas_call(
        functools.partial(adam_step, xs * zs * cores),
        out_shape=(block, block, block, jax.ShapeDtypeStruct((zs, sent_rows, LANES), BF16)),
        in_specs=[SMEM, SMEM] + [VMEM] * 5,
        out_specs=(VMEM,) * 4,
        compiler_params=grant(4),
    )(place, moment_range, value, top, master, moment_q, second_moment)

    held = lax.all_to_all(held, "z", 0, 0, tiled=True)
    held = pl.pallas_call(
        join_blocks,
        out_shape=jax.ShapeDtypeStruct((zs * packed + TOP_ROWS, LANES), BF16),
        in_specs=[VMEM],
        out_specs=VMEM,
        compiler_params=grant(4),
    )(held)
    held = lax.all_gather(held, "x")
    other = lax.ppermute(held, "core", swap)
    tops = pl.pallas_call(
        join_tops,
        out_shape=jax.ShapeDtypeStruct((cores * ys, 8, LANES), F32),
        in_specs=[VMEM],
        out_specs=VMEM,
        compiler_params=grant(4),
    )(held)
    tops = lax.all_to_all(tops, ("core", "y"), 0, 0, tiled=True)

    one = jax.ShapeDtypeStruct((1,), F32)
    weight_q, moment_q_new, moment_span, weight_span, grad_span = pl.pallas_call(
        scale_weights,
        grid=(xs,),
        out_shape=(
            jax.ShapeDtypeStruct((rows, width * xs * zs * cores), BF16),
            jax.ShapeDtypeStruct((rows, width), BF16),
            one,
            one,
            one,
        ),
        in_specs=[SMEM, VMEM, VMEM, VMEM, VMEM],
        out_specs=(
            pl.BlockSpec((rows, width * zs * cores), lambda i: (0, i)),
            VMEM,
            SMEM,
            SMEM,
            SMEM,
        ),
        scratch_shapes=[pltpu.VMEM((8, LANES), F32)],
        compiler_params=grant(8),
    )(place, tops, held, other, moment)
    return master_new, moment_q_new, moment_span, second_new, weight_q, weight_span, grad_span


def solution(mesh):
    inner = Mesh(mesh.devices.reshape(4, 8, 2, 8), DEVICE)
    dp, mp = ("x", "z", "core"), "y"
    placed = (P(dp, mp), P(dp, mp), P(mp, dp), P(mp, dp), P(), P(mp, dp))
    return jax.shard_map(
        on_device,
        mesh=inner,
        in_specs=placed,
        out_specs=(P(mp, dp), P(mp, dp), P(), P(mp, dp), P(mp, None), P(), P()),
        check_vma=False,
    )
```
